32 devices in a mesh: dp: 2 (over y), seq: 16 (over z, x, core).
Axes of the slice: x: 2, y: 2, z: 4, core: 2. Of those that a mesh axis runs over, the one named last changes fastest.
Arguments:
- mel_frames: bfloat16 [2, 4096, 128], P('dp', 'seq'), may hold values from -6 to 6
- positions: int32 [2, 2048], P('dp', 'seq'), may hold values from 0 to 4095, as said below
- conv_weight: bfloat16 [128, 3, 1280], replicated, may hold values from -0.3125 to 0.3125
- conv_bias: float32 [1280], replicated, may hold values from -3 to 3
- proj_weight: bfloat16 [1280, 2048], P('dp'), may hold values from -0.15625 to 0.15625
- proj_bias: float32 [2048], replicated, may hold values from -3 to 3
- cotangent: bfloat16 [2, 4096, 2048], P('dp', 'seq'), may hold values from -0.13183594 to 0.13183594
Outputs:
- merged: bfloat16 [2, 4096, 2048], P('dp', 'seq')
- grad_weight: float32 [128, 3, 1280], P('seq', None, 'dp')
The draws below stay inside these ranges and needn't reach their ends.
Inputs may be any that keep to these rules, and one draw needn't show every extreme that they name: Within a recording the 2048 entries are distinct. Block b of the sequence is positions b * 256 to b * 256 + 255; the 128 tokens of one window put at most 16 entries into any one block, and in each recording one block receives exactly 16 from every window.
All inputs are finite; a program needn't handle non-finite values.
Results may differ from the reference program's by a relative error of at most 0.012.
Values may be sent and summed in bfloat16 or wider, within the bound.
No kernel may reach another device: no remote copies, remote signals or barrier semaphores. Data moves between devices by JAX's collectives and lax.ppermute only.
A program may use at most 64 MiB of HBM per device.

```python
import jax
import jax.numpy as jnp
from jax import lax

NMEL = 128
KW = 3
CH = 1280
D = 2048
FRAMES = 256
TOK = 128
CAP = 16
ROWS_OWN = 256
RECS = 2
SEQ_FRAMES = 4096
TOKENS = 2048
SEQ_LEN = 4096
ALL_FRAMES = 8192
N_DP = 2
N_SEQ = 16


def owner_permutation(row_key):
    return jax.random.permutation(row_key, ROWS_OWN).astype(jnp.int32)


def record_positions(record_key):
    key_full, key_rows, key_sources = jax.random.split(record_key, 3)
    full_owner = jax.random.randint(key_full, (), 0, N_SEQ).astype(jnp.int32)
    slot_total = N_SEQ * CAP
    slot_ids = jnp.arange(slot_total, dtype=jnp.int32)
    slot_owner = slot_ids // CAP
    row_tables = jax.vmap(owner_permutation)(jax.random.split(key_rows, N_SEQ))
    source_keys = jax.random.split(key_sources, N_SEQ)

    def one_source(source_index, source_key):
        key_scores, key_order = jax.random.split(source_key)
        scores = jax.random.permutation(key_scores, slot_total).astype(jnp.int32)
        scores = jnp.where(slot_owner == full_owner, slot_ids - slot_total, scores)
        sorted_slots = jnp.argsort(scores).astype(jnp.int32)
        kept_slots = sorted_slots[:TOK]
        kept_slots = kept_slots[jax.random.permutation(key_order, TOK)]
        owners = kept_slots // CAP
        local_slot = source_index * CAP + kept_slots % CAP
        owner_rows = row_tables[owners, local_slot]
        return owners * ROWS_OWN + owner_rows
    result = jax.vmap(one_source)(jnp.arange(N_SEQ, dtype=jnp.int32), source_keys)
    return result.reshape(-1)


def draw_positions(key, part):
    record_keys = jax.random.split(key, N_DP)
    return jax.vmap(record_positions)(record_keys).astype(jnp.int32)


def with_spikes(drawn, rng, source, target, parts, factor):
    owner, partner = [(jnp.arange(drawn.shape[axis_at]) // (drawn.shape[axis_at] // parts)).reshape([-1 if axis == axis_at else 1 for axis in range(drawn.ndim)]) for axis_at in (source, target)]
    chosen = jax.random.permutation(rng, parts)[partner]
    strong = (owner == chosen) | (owner == (partner + parts // 2) % parts)
    return jnp.where(strong, factor * drawn, drawn)


def level_of(key, shape, cuts, low, high):
    def one(position, shards_of):
        heights = jax.random.uniform(jax.random.fold_in(jax.random.fold_in(key, 6), position), (shards_of,), jnp.float32, low / len(cuts), high / len(cuts))
        return jnp.repeat(jnp.exp(heights), shape[position] // shards_of).reshape((-1,) + (1,) * (len(shape) - position - 1))

    gain = one(*cuts[0])
    for cut in cuts[1:]:
        gain = gain * one(*cut)
    return gain


def scatter_about(own_key, extent, spread, reach, pieces=(), held_as=jnp.bfloat16):
    values = spread * jax.random.normal(own_key, extent, jnp.float32)
    if pieces:
        values = values * level_of(own_key, extent, pieces, -0.22, 0.18)
    return jnp.clip(values, -reach, reach).astype(held_as)


def noise_with(rng, extent, deviation, most, cuts, heavy, kind=jnp.bfloat16):
    drawn = deviation * jax.random.normal(rng, extent, jnp.float32)
    if cuts:
        drawn = drawn * level_of(rng, extent, cuts, -0.22, 0.18)
    return jnp.clip(with_spikes(drawn, jax.random.fold_in(rng, 3), *heavy), -most, most).astype(kind)


def setup_inputs(seed: int = 0) -> dict:
    keys = jax.random.split(jax.random.key(seed), 8)
    mel_frames = noise_with(keys[0], (RECS, SEQ_FRAMES, NMEL), 1.0, 6.0, ((0, 2), (1, 16)), (1, 2, 16, 2.0))
    positions = draw_positions(jax.random.fold_in(keys[7], 71), 0)
    conv_weight = scatter_about(keys[2], (NMEL, KW, CH), (NMEL * KW) ** -0.5, 0.3125)
    conv_bias = scatter_about(keys[3], (CH,), 0.5, 3.0, (), jnp.float32)
    proj_weight = scatter_about(keys[4], (CH, D), CH ** -0.5, 0.15625, ((0, 2),))
    proj_bias = scatter_about(keys[5], (D,), 0.5, 3.0, (), jnp.float32)
    cotangent = scatter_about(keys[6], (RECS, SEQ_LEN, D), (2.0 / ALL_FRAMES ** 0.5), 0.13183594, ((0, 2), (1, 16)))
    return {"mel_frames": mel_frames, "positions": positions, "conv_weight": conv_weight, "conv_bias": conv_bias, "proj_weight": proj_weight, "proj_bias": proj_bias, "cotangent": cotangent}


SQRT_HALF = 0.7071067811865476
INV_SQRT_TWO_PI = 0.3989422804014327


def gelu_value(x):
    return x * 0.5 * (1.0 + lax.erf(x * SQRT_HALF))


def gelu_slope(x):
    return 0.5 * (1.0 + lax.erf(x * SQRT_HALF)) + x * INV_SQRT_TWO_PI * jnp.exp(-0.5 * x * x)


def reference(mel_frames, positions, conv_weight, conv_bias, proj_weight, proj_bias, cotangent):
    kernel = jnp.transpose(conv_weight, (1, 0, 2)).reshape(KW * NMEL, CH)

    def one_record(record_args):
        frames, token_spots, grads_in = record_args
        windows = frames.reshape(N_SEQ, FRAMES, NMEL)
        padded = jnp.pad(windows, ((0, 0), (1, 1), (0, 0)))
        stacked = jnp.concatenate([padded[:, k:k + FRAMES, :] for k in range(KW)], axis=2)
        stacked = stacked.reshape(N_SEQ * FRAMES, KW * NMEL)
        pre_act = jnp.dot(stacked, kernel, preferred_element_type=jnp.float32) + conv_bias
        act_pairs = gelu_value(pre_act).reshape(TOKENS, 2, CH)
        pooled = (0.5 * (act_pairs[:, 0, :] + act_pairs[:, 1, :])).astype(jnp.bfloat16)
        projected = (jnp.dot(pooled, proj_weight, preferred_element_type=jnp.float32) + proj_bias).astype(jnp.bfloat16)
        merged = jnp.zeros((SEQ_LEN, D), jnp.bfloat16).at[token_spots].set(projected)
        grad_tokens = jnp.take(grads_in, token_spots, axis=0)
        grad_pooled = jnp.dot(grad_tokens, proj_weight.T, preferred_element_type=jnp.float32).astype(jnp.bfloat16)
        slopes = gelu_slope(pre_act).reshape(TOKENS, 2, CH)
        grad_pre = (0.5 * grad_pooled.astype(jnp.float32)[:, None, :] * slopes).astype(jnp.bfloat16)
        grad_pre = grad_pre.reshape(N_SEQ * FRAMES, CH)
        tap_terms = []
        for k in range(KW):
            shifted = padded[:, k:k + FRAMES, :].reshape(N_SEQ * FRAMES, NMEL)
            tap_terms.append(jnp.dot(shifted.T, grad_pre, preferred_element_type=jnp.float32))
        return merged, jnp.stack(tap_terms, axis=1)

    merged, record_terms = lax.map(one_record, (mel_frames, positions, cotangent))
    return merged, jnp.sum(record_terms, axis=0)
```

```python
import functools

import jax
import jax.numpy as jnp
from jax import lax
from jax.experimental import pallas as pl
from jax.experimental.pallas import tpu as pltpu
from jax.sharding import PartitionSpec as P

SQRT_HALF = 0.7071067811865476
INV_SQRT_TWO_PI = 0.3989422804014327
META_ROWS = 16
LANES = 128
VMEM_LIMIT = 48 * 1024 * 1024
F32, BF16, I32 = jnp.float32, jnp.bfloat16, jnp.int32


def iota(shape, dim):
    return lax.broadcasted_iota(I32, shape, dim)


def mm(a, b):
    return jnp.dot(a, b, preferred_element_type=F32)


def pack_kernel(owners, capacity, rows_own, *refs):
    bufs, out = refs[:-1], refs[-1]
    slots = owners * capacity
    frames = bufs[0].shape[0] - META_ROWS
    mel = bufs[0].shape[1]
    toks = frames // 2
    before = (iota((toks, toks), 0) < iota((toks, toks), 1)).astype(F32).astype(BF16)
    lane = iota((slots, LANES), 1)
    meta_out = jnp.zeros((slots, LANES), F32)
    for j, buf in enumerate(bufs):
        meta = buf[frames : frames + META_ROWS, :].astype(F32)
        owner, row = meta[0:1, :].astype(I32), meta[1:2, :]
        mine = (iota((owners, toks), 0) == owner).astype(F32)
        ahead = mm(mine.astype(BF16), before)
        rank = jnp.sum(mine * ahead, axis=0, keepdims=True).astype(I32)
        onehot = (iota((slots, toks), 0) == owner * capacity + rank).astype(F32)
        spot = jnp.sum(onehot * (row - rows_own), axis=1, keepdims=True) + rows_own
        meta_out = jnp.where(lane == j, spot, meta_out)
        onehot = onehot.astype(BF16)
        window = buf[0:frames, :]
        for k in range(4):
            pick = (iota((toks, frames), 1) == 2 * iota((toks, frames), 0) - 1 + k).astype(F32)
            part = mm(pick.astype(BF16), window).astype(BF16)
            left = (j * 4 + k) * mel
            out[:, left : left + mel] = mm(onehot, part).astype(BF16)
    out[:, len(bufs) * 4 * mel :] = meta_out.astype(BF16)


def rows_from_slots(arrived, meta, j, rows):
    spots = jnp.transpose(meta.astype(F32)).astype(I32)
    spots = jnp.sum(jnp.where(iota(spots.shape, 0) == j, spots, 0), axis=0, keepdims=True)
    onehot = (iota((rows, spots.shape[1]), 0) == spots).astype(F32)
    return mm(onehot.astype(BF16), arrived).astype(BF16), onehot


def halves(patch, kernel, bias):
    depth = kernel.shape[0]
    mel = patch.shape[1] // 4
    return mm(patch[:, :depth], kernel) + bias, mm(patch[:, mel:], kernel) + bias


def cdf_of(x):
    return 0.5 * (1.0 + lax.erf(x * SQRT_HALF))


def slope_of(x, cdf):
    return cdf + x * INV_SQRT_TWO_PI * jnp.exp(-0.5 * x * x)


def forward_kernel(arrived, meta, kernel, bias, weight, out):
    rows = out.shape[1]
    patch, _ = rows_from_slots(arrived[...], meta[...], pl.program_id(0) + 1, rows)
    even, odd = halves(patch, kernel[...], bias[...])
    pooled = (0.5 * (even * cdf_of(even) + odd * cdf_of(odd))).astype(BF16)
    out[0] = mm(pooled, weight[...]).astype(BF16)


def backward_kernel(arrived, meta, kernel, bias, weight, grads, grad_out, own_out, valid_out):
    j = pl.program_id(0)
    rows = grads.shape[1]
    patch, onehot = rows_from_slots(arrived[...], meta[...], j, rows)
    even, odd = halves(patch, kernel[...], bias[...])
    even_cdf, odd_cdf = cdf_of(even), cdf_of(odd)

    @pl.when(j == 0)
    def _():
        pooled = (0.5 * (even * even_cdf + odd * odd_cdf)).astype(BF16)
        own_out[...] = mm(pooled, weight[...])
        valid_out[...] = jnp.broadcast_to(jnp.sum(onehot, axis=1, keepdims=True), valid_out.shape)
        grad_out[...] = jnp.zeros_like(grad_out)

    half = 0.5 * grads[0].astype(F32)
    even_grad = (half * slope_of(even, even_cdf)).astype(BF16)
    odd_grad = (half * slope_of(odd, odd_cdf)).astype(BF16)
    depth = kernel.shape[0]
    mel = patch.shape[1] // 4
    first = (((0,), (0,)), ((), ()))
    grad_out[...] += lax.dot_general(
        patch[:, :depth], even_grad, first, preferred_element_type=F32
    ) + lax.dot_general(patch[:, mel:], odd_grad, first, preferred_element_type=F32)


def body(mel_frames, positions, conv_weight, conv_bias, proj_weight, proj_bias, cotangent):
    recs, owners = lax.axis_size("dp"), lax.axis_size("seq")
    dp_index, seq_index = lax.axis_index("dp"), lax.axis_index("seq")
    frames, mel = mel_frames.shape[1:]
    toks = positions.shape[1]
    rows, feats = cotangent.shape[1:]
    capacity = rows // owners
    slots = owners * capacity
    taps = conv_weight.shape[1]
    chans = proj_weight.shape[0]
    assert taps == 3 and toks == LANES == mel and frames == 2 * toks and rows <= 256

    def shift(x, by):
        return lax.ppermute(x, "dp", [(i, (i + by) % recs) for i in range(recs)])

    spots = positions[0][None, :]
    meta = jnp.concatenate(
        [spots // rows, spots % rows, jnp.zeros((META_ROWS - 2, toks), I32)], axis=0
    ).astype(BF16)
    buf = jnp.concatenate([mel_frames[0], meta], axis=0)
    bufs = [buf] + [shift(buf, j) for j in range(1, recs)]
    cots = [cotangent[0]] + [shift(cotangent[0], j) for j in range(1, recs)]

    width = recs * 4 * mel + LANES
    packed = pl.pallas_call(
        functools.partial(pack_kernel, owners, capacity, rows),
        out_shape=jax.ShapeDtypeStruct((slots, width), BF16),
        compiler_params=pltpu.CompilerParams(vmem_limit_bytes=VMEM_LIMIT),
        name="pack_patches",
    )(*bufs)
    arrived = lax.all_to_all(
        packed.reshape(owners, capacity, width), "seq", split_axis=0, concat_axis=0, tiled=True
    ).reshape(slots, width)

    kernel = lax.dynamic_slice_in_dim(conv_weight, dp_index * chans, chans, 2)
    kernel = jnp.transpose(kernel, (1, 0, 2)).reshape(taps * mel, chans)
    bias = lax.dynamic_slice_in_dim(conv_bias, dp_index * chans, chans, 0)[None, :]

    whole = lambda *shape: pl.BlockSpec(shape, lambda j: (0,) * len(shape))
    partial = pl.pallas_call(
        forward_kernel,
        grid=(recs - 1,),
        in_specs=[
            pl.BlockSpec((slots, 4 * mel), lambda j: (0, j + 1)),
            pl.BlockSpec((slots, LANES), lambda j: (0, recs * 4 * mel // LANES)),
            whole(taps * mel, chans),
            whole(1, chans),
            whole(chans, feats),
        ],
        out_specs=pl.BlockSpec((1, rows, feats), lambda j: (j, 0, 0)),
        out_shape=jax.ShapeDtypeStruct((recs - 1, rows, feats), BF16),
        compiler_params=pltpu.CompilerParams(vmem_limit_bytes=VMEM_LIMIT),
        name="forward_partial",
    )(arrived, arrived, kernel, bias, proj_weight)
    returned = [shift(partial[j - 1], -j) for j in range(1, recs)]

    contract_last = (((1,), (1,)), ((), ()))
    grads = jnp.stack(
        [
            lax.dot_general(c, proj_weight, contract_last, preferred_element_type=F32).astype(BF16)
            for c in cots
        ]
    )
    grad_part, own, valid = pl.pallas_call(
        backward_kernel,
        grid=(recs,),
        in_specs=[
            pl.BlockSpec((slots, 4 * mel), lambda j: (0, j)),
            pl.BlockSpec((slots, LANES), lambda j: (0, recs * 4 * mel // LANES)),
            whole(taps * mel, chans),
            whole(1, chans),
            whole(chans, feats),
            pl.BlockSpec((1, rows, chans), lambda j: (j, 0, 0)),
        ],
        out_specs=[whole(taps * mel, chans), whole(rows, feats), whole(rows, LANES)],
        out_shape=[
            jax.ShapeDtypeStruct((taps * mel, chans), F32),
            jax.ShapeDtypeStruct((rows, feats), F32),
            jax.ShapeDtypeStruct((rows, LANES), F32),
        ],
        compiler_params=pltpu.CompilerParams(vmem_limit_bytes=VMEM_LIMIT),
        name="backward",
    )(arrived, arrived, kernel, bias, proj_weight, grads)

    total = own
    for part in returned:
        total = total + part.astype(F32)
    merged = jnp.where(valid[:, :1] > 0.0, total + proj_bias, 0.0).astype(BF16)

    share = mel // owners
    split = grad_part.reshape(taps, owners // 2, 2, share, chans)
    core = seq_index % 2
    keep = lax.dynamic_index_in_dim(split, core, 2, keepdims=False)
    send = lax.dynamic_index_in_dim(split, 1 - core, 2, keepdims=False).astype(BF16)
    got = lax.ppermute(send, "seq", [(i, i ^ 1) for i in range(owners)])
    pair = (keep + got.astype(F32)).astype(BF16)
    pair = jnp.transpose(pair, (1, 0, 2, 3)).reshape(owners // 2, taps * share, chans)
    groups = [list(range(c, owners, 2)) for c in range(2)]
    pieces = lax.all_to_all(
        pair, "seq", split_axis=0, concat_axis=0, axis_index_groups=groups, tiled=True
    )
    grad_weight = jnp.sum(pieces.astype(F32), axis=0).reshape(taps, share, chans)
    return merged[None], jnp.transpose(grad_weight, (1, 0, 2))


def solution(mesh):
    in_specs = (
        P("dp", "seq", None),
        P("dp", "seq"),
        P(),
        P(),
        P("dp", None),
        P(),
        P("dp", "seq", None),
    )
    out_specs = (P("dp", "seq", None), P("seq", None, "dp"))
    return jax.shard_map(body, mesh=mesh, in_specs=in_specs, out_specs=out_specs, check_vma=False)
```

```python
import functools

import jax
import jax.numpy as jnp
from jax import lax
from jax.experimental import pallas as pl
from jax.experimental.pallas import tpu as pltpu
from jax.sharding import PartitionSpec as P

SQRT_HALF = 0.7071067811865476
INV_SQRT_TWO_PI = 0.3989422804014327
LANES = 128
VMEM_LIMIT = 48 * 1024 * 1024
F32, BF16, I32 = jnp.float32, jnp.bfloat16, jnp.int32


def iota(shape, dim):
    return lax.broadcasted_iota(I32, shape, dim)


def mm(a, b):
    return jnp.dot(a, b, preferred_element_type=F32)


def call(kernel, out_shape, name, **kwargs):
    return pl.pallas_call(
        kernel,
        out_shape=out_shape,
        compiler_params=pltpu.CompilerParams(vmem_limit_bytes=VMEM_LIMIT),
        name=name,
        **kwargs,
    )


def pack_kernel(owners, capacity, rows_own, mel_ref, spots_ref, out):
    slots = owners * capacity
    frames, mel = mel_ref.shape
    toks = frames // 2
    spots = spots_ref[...]
    owner = spots // rows_own
    row = spots - owner * rows_own
    before = (iota((toks, toks), 0) < iota((toks, toks), 1)).astype(F32).astype(BF16)
    mine = (iota((owners, toks), 0) == owner).astype(F32)
    ahead = mm(mine.astype(BF16), before)
    rank = jnp.sum(mine * ahead, axis=0, keepdims=True).astype(I32)
    onehot = (iota((slots, toks), 0) == owner * capacity + rank).astype(F32)
    spot = jnp.sum(onehot * (row - rows_own).astype(F32), axis=1, keepdims=True) + rows_own
    onehot = onehot.astype(BF16)
    window = mel_ref[...]
    for k in range(4):
        pick = (iota((toks, frames), 1) == 2 * iota((toks, frames), 0) - 1 + k).astype(F32)
        part = mm(pick.astype(BF16), window).astype(BF16)
        out[:, k * mel : (k + 1) * mel] = mm(onehot, part).astype(BF16)
    out[:, 4 * mel :] = jnp.broadcast_to(spot, (slots, LANES)).astype(BF16)


def rows_from_slots(arrived, rows):
    width = arrived.shape[1] - LANES
    spots = jnp.transpose(arrived[:, width:].astype(F32))[0:1, :].astype(I32)
    onehot = (iota((rows, spots.shape[1]), 0) == spots).astype(F32)
    return mm(onehot.astype(BF16), arrived[:, :width]).astype(BF16), onehot


def activation_kernel(own, other, kernel, bias, order, pooled_out, slope_out, left_out, valid_out):
    rows = pooled_out.shape[1]
    depth = kernel.shape[0]
    for n, ref in enumerate((own, other)):
        patch, onehot = rows_from_slots(ref, rows)
        if n == 0:
            valid_out[...] = jnp.broadcast_to(
                jnp.sum(onehot, axis=1, keepdims=True), valid_out.shape
            )
        mel = patch.shape[1] // 4
        acts = []
        for p in range(2):
            frames = patch[:, p * mel : p * mel + depth]
            left_out[n, p] = mm(frames, order[...]).astype(BF16)
            x = mm(frames, kernel[...]) + bias[...]
            cdf = 0.5 * (1.0 + lax.erf(x * SQRT_HALF))
            acts.append(x * cdf)
            slope_out[n, p] = 0.5 * (cdf + x * INV_SQRT_TWO_PI * jnp.exp(-0.5 * x * x))
        pooled_out[n] = (0.5 * (acts[0] + acts[1])).astype(BF16)


def assemble(offsets, weights, whole):
    for n, ref in enumerate(weights):
        start = pl.multiple_of(offsets[n], 16)
        whole[pl.ds(start, ref.shape[0]), :] = ref[...]


def backward_kernel(offsets, halves, cot_own, cot_other, slope, left, *refs):
    weights, out, whole = refs[:-2], refs[-2], refs[-1]
    assemble(offsets, weights, whole)
    first = (((0,), (0,)), ((), ()))
    last = (((1,), (1,)), ((), ()))
    total = None
    for n, cot in enumerate((cot_own, cot_other)):
        grads = lax.dot_general(cot[...], whole[...], last, preferred_element_type=F32)
        grads = grads.astype(BF16).astype(F32)
        for p in range(2):
            pre = (grads * slope[n, p]).astype(BF16)
            term = lax.dot_general(left[n, p], pre, first, preferred_element_type=F32)
            total = term if total is None else total + term
    share = out.shape[2]
    for j in range(out.shape[0]):
        out[halves[j]] = total[:, j * share : (j + 1) * share].astype(BF16)


def forward_kernel(offsets, pooled, *refs):
    weights, other_out, own_out, whole = refs[:-3], refs[-3], refs[-2], refs[-1]
    assemble(offsets, weights, whole)
    other_out[...] = mm(pooled[1], whole[...]).astype(BF16)
    own_out[...] = mm(pooled[0], whole[...])


def body(mel_frames, positions, conv_weight, conv_bias, proj_weight, proj_bias, cotangent):
    recs, owners = lax.axis_size("dp"), lax.axis_size("seq")
    dp_index, seq_index = lax.axis_index("dp"), lax.axis_index("seq")
    core, side = seq_index % 2, (seq_index // 2) % 2
    frames, mel = mel_frames.shape[1:]
    toks = positions.shape[1]
    rows, feats = cotangent.shape[1:]
    capacity = rows // owners
    slots = owners * capacity
    taps = conv_weight.shape[1]
    depth = taps * mel
    chans = proj_weight.shape[0]
    quarter = chans // 2
    width = recs * quarter
    assert taps == 3 and toks == LANES == mel and frames == 2 * toks and rows <= 256

    def shift(x, by):
        return lax.ppermute(x, "dp", [(i, (i + by) % recs) for i in range(recs)])

    def swap(x, bit):
        return lax.ppermute(x, "seq", [(i, i ^ bit) for i in range(owners)])

    end = quarter * 7 // 20 // 16 * 16
    middle = quarter - 2 * end
    base = core * quarter
    head = lax.dynamic_slice_in_dim(proj_weight, base + side * (end + middle), end, 0)
    mid = lax.dynamic_slice_in_dim(proj_weight, base + end, middle, 0)
    own_rows = lax.dynamic_slice_in_dim(proj_weight, base, quarter, 0)
    weights, offsets = [own_rows], [0]
    heads = [shift(head, j) for j in range(1, recs)]
    mids = [shift(mid, j) for j in range(1, recs)]
    tails = [swap(h, 2) for h in heads]
    for j in range(1, recs):
        weights += [heads[j - 1], mids[j - 1], tails[j - 1]]
        at = j * quarter
        offsets += [at + side * (end + middle), at + end, at + (1 - side) * (end + middle)]
    offsets = jnp.stack([jnp.asarray(o, I32) for o in offsets])
    halves = jnp.stack([(dp_index - j) % recs for j in range(recs)]).astype(I32)
    smem = pl.BlockSpec(memory_space=pltpu.SMEM)
    vmem = pl.BlockSpec(memory_space=pltpu.VMEM)

    cot_own = cotangent[0]
    cot_other = swap(cot_own, 1)

    packed = call(
        functools.partial(pack_kernel, owners, capacity, rows),
        jax.ShapeDtypeStruct((slots, 4 * mel + LANES), BF16),
        "pack_patches",
    )(mel_frames[0], positions)
    arrived = lax.all_to_all(
        packed.reshape(owners, capacity, -1), "seq", split_axis=0, concat_axis=0, tiled=True
    ).reshape(slots, -1)
    arrived_other = swap(arrived, 1)

    def mine(x):
        x = x.reshape(x.shape[0], recs, 2, quarter)
        x = lax.dynamic_index_in_dim(x, core, 2, keepdims=False)
        return jnp.concatenate(
            [lax.dynamic_index_in_dim(x, halves[j], 1, keepdims=False) for j in range(recs)], axis=1
        )

    kernel = mine(jnp.transpose(conv_weight, (1, 0, 2)).reshape(depth, -1))
    bias = mine(conv_bias[None, :])
    share = mel // owners
    target = jnp.arange(depth)
    target = (target // share % taps) * mel + target // (taps * share) * share + target % share
    order = (jnp.arange(depth)[:, None] == target[None, :]).astype(BF16)

    pooled, slope, left, valid = call(
        activation_kernel,
        [
            jax.ShapeDtypeStruct((2, rows, width), BF16),
            jax.ShapeDtypeStruct((2, 2, rows, width), F32),
            jax.ShapeDtypeStruct((2, 2, rows, depth), BF16),
            jax.ShapeDtypeStruct((rows, LANES), F32),
        ],
        "activations",
    )(arrived, arrived_other, kernel, bias, order)

    whole = pltpu.VMEM((width, feats), BF16)
    sums = call(
        backward_kernel,
        jax.ShapeDtypeStruct((recs, depth, quarter), BF16),
        "backward",
        in_specs=[smem, smem] + [vmem] * (4 + len(weights)),
        scratch_shapes=[whole],
    )(offsets, halves, cot_own, cot_other, slope, left, *weights)
    pieces = lax.all_to_all(
        sums.reshape(recs * owners, taps * share, quarter),
        ("dp", "seq"),
        split_axis=0,
        concat_axis=0,
        tiled=True,
    )
    pieces = pieces.reshape(recs * owners // 2, 2, taps * share, quarter)
    grad_weight = jnp.sum(pieces.astype(F32), axis=0)
    grad_weight = jnp.transpose(grad_weight, (1, 0, 2)).reshape(taps, share, chans)

    partial, own = call(
        forward_kernel,
        [
            jax.ShapeDtypeStruct((rows, feats), BF16),
            jax.ShapeDtypeStruct((rows, feats), F32),
        ],
        "forward",
        in_specs=[smem] + [vmem] * (1 + len(weights)),
        scratch_shapes=[whole],
    )(offsets, pooled, *weights)
    total = own + swap(partial, 1).astype(F32) + proj_bias
    merged = jnp.where(valid[:, :1] > 0.0, total, 0.0).astype(BF16)
    return merged[None], jnp.transpose(grad_weight, (1, 0, 2))


def solution(mesh):
    in_specs = (
        P("dp", "seq", None),
        P("dp", "seq"),
        P(),
        P(),
        P("dp", None),
        P(),
        P("dp", "seq", None),
    )
    out_specs = (P("dp", "seq", None), P("seq", None, "dp"))
    return jax.shard_map(body, mesh=mesh, in_specs=in_specs, out_specs=out_specs, check_vma=False)
```

```python
import functools

import jax
import jax.numpy as jnp
from jax import lax
from jax.experimental import pallas as pl
from jax.experimental.pallas import tpu as pltpu
from jax.sharding import PartitionSpec as P

SQRT_HALF = 0.7071067811865476
INV_SQRT_TWO_PI = 0.3989422804014327
LANES = 128
VMEM_LIMIT = 16 * 1024 * 1024
HBM = pltpu.MemorySpace.HBM
F32, BF16, I32 = jnp.float32, jnp.bfloat16, jnp.int32


def iota(shape, dim):
    return lax.broadcasted_iota(I32, shape, dim)


def mm(a, b):
    return jnp.dot(a, b, preferred_element_type=F32)


def call(kernel, out_shape, name, micros=1, **kwargs):
    cost = pl.CostEstimate(flops=micros * 10**9, bytes_accessed=0, transcendentals=0)
    return pl.pallas_call(
        kernel,
        out_shape=out_shape,
        compiler_params=pltpu.CompilerParams(vmem_limit_bytes=VMEM_LIMIT),
        cost_estimate=cost,
        name=name,
        **kwargs,
    )


def in_hbm(x):
    return pltpu.with_memory_space_constraint(x, HBM)


def fetch(copies):
    for copy in copies:
        copy.start()


def settle(copies):
    for copy in copies:
        copy.wait()


def pack_kernel(owners, capacity, rows_own, mel_hbm, spots_hbm, out, mel_ref, spots_ref, sems):
    loads = [
        pltpu.make_async_copy(spots_hbm, spots_ref, sems.at[0]),
        pltpu.make_async_copy(mel_hbm, mel_ref, sems.at[1]),
    ]
    fetch(loads)
    slots = owners * capacity
    frames, mel = mel_ref.shape
    toks = frames // 2
    settle(loads)
    spots = spots_ref[...]
    owner = spots // rows_own
    row = spots - owner * rows_own
    before = (iota((toks, toks), 0) < iota((toks, toks), 1)).astype(F32).astype(BF16)
    mine = (iota((owners, toks), 0) == owner).astype(F32)
    ahead = mm(mine.astype(BF16), before)
    rank = jnp.sum(mine * ahead, axis=0, keepdims=True).astype(I32)
    onehot = (iota((slots, toks), 0) == owner * capacity + rank).astype(F32)
    spot = jnp.sum(onehot * (row - rows_own).astype(F32), axis=1, keepdims=True) + rows_own
    onehot = onehot.astype(BF16)
    window = mel_ref[...]
    for k in range(4):
        pick = (iota((toks, frames), 1) == 2 * iota((toks, frames), 0) - 1 + k).astype(F32)
        part = mm(pick.astype(BF16), window).astype(BF16)
        out[:, k * mel : (k + 1) * mel] = mm(onehot, part).astype(BF16)
    out[:, 4 * mel :] = jnp.broadcast_to(spot, (slots, LANES)).astype(BF16)


def rows_from_slots(arrived, rows):
    width = arrived.shape[1] - LANES
    spots = jnp.transpose(arrived[:, width:].astype(F32))[0:1, :].astype(I32)
    onehot = (iota((rows, spots.shape[1]), 0) == spots).astype(F32)
    return mm(onehot.astype(BF16), arrived[:, :width]).astype(BF16), onehot


LAST = (((1,), (1,)), ((), ()))


def ordered(frames, taps, share):
    depth = frames.shape[1]
    mel = depth // taps
    row = iota((depth, 1), 0).astype(F32)
    block = jnp.floor((row + 0.5) / (taps * share))
    within = row - block * (taps * share)
    tap = jnp.floor((within + 0.5) / share)
    source = (tap * mel + block * share + within - tap * share).astype(I32)
    order = (iota((depth, depth), 1) == source).astype(F32).astype(BF16)
    return lax.dot_general(order, frames, LAST, preferred_element_type=F32).astype(BF16)


def activations(frames, kernel, bias, rows):
    acts = mm(frames, kernel) + bias
    pool, slopes = None, []
    for p in range(2):
        x = acts[p * rows : (p + 1) * rows]
        cdf = 0.5 * (1.0 + lax.erf(x * SQRT_HALF))
        act = x * cdf
        pool = act if pool is None else pool + act
        slopes.append(0.5 * (cdf + x * INV_SQRT_TWO_PI * jnp.exp(-0.5 * x * x)))
    return (0.5 * pool).astype(BF16), slopes


def both_frames(patch, depth):
    mel = patch.shape[1] // 4
    return jnp.concatenate([patch[:, p * mel : p * mel + depth] for p in range(2)], axis=0)


def prepare_kernel(share, base, offsets, arrived, kernel, bias, own_in, other_in, weight_in, *refs):
    heads, (cots, whole, left, slopes, pooled, valid, sems) = refs[:-7], refs[-7:]
    rows = pooled.shape[0]
    depth = kernel.shape[0]
    quarter = whole.shape[0] // (len(heads) + 1)
    start = pl.multiple_of(base[0], 16)
    loads = [
        pltpu.make_async_copy(own_in, cots.at[pl.ds(0, rows)], sems.at[0]),
        pltpu.make_async_copy(other_in, cots.at[pl.ds(rows, rows)], sems.at[1]),
        pltpu.make_async_copy(
            weight_in.at[pl.ds(start, quarter)], whole.at[pl.ds(0, quarter)], sems.at[2]
        ),
    ]
    fetch(loads)
    place(offsets, heads, whole)
    patch, onehot = rows_from_slots(arrived[...], rows)
    valid[...] = jnp.broadcast_to(jnp.sum(onehot, axis=1, keepdims=True), valid.shape)
    frames = both_frames(patch, depth)
    left[...] = ordered(frames, depth // (patch.shape[1] // 4), share)
    pooled[...], halves = activations(frames, kernel[...], bias[...], rows)
    for p in range(2):
        slopes[p] = halves[p]
    settle(loads)


def place(offsets, weights, whole):
    for n, ref in enumerate(weights):
        start = pl.multiple_of(offsets[n], 16)
        whole[pl.ds(start, ref.shape[0]), :] = ref[...]


def backward_kernel(share, offsets, halves, cots, whole_in, left, slopes, kernel, bias, arrived, *refs):
    weights, (sums_out, pooled_out, whole, sums, pooled, sems) = refs[:-6], refs[-6:]
    rows = pooled.shape[0]
    depth = kernel.shape[0]
    place(offsets, weights, whole)
    patch, _ = rows_from_slots(arrived[...], rows)
    frames = both_frames(patch, depth)
    other_left = ordered(frames, depth // (patch.shape[1] // 4), share)
    pooled[...], other_slopes = activations(frames, kernel[...], bias[...], rows)
    stores = [pltpu.make_async_copy(pooled, pooled_out, sems.at[0])]
    stores[0].start()
    grads = lax.dot_general(cots[...], whole[...], LAST, preferred_element_type=F32)
    grads = grads.astype(BF16).astype(F32)
    pres = [grads[:rows] * slopes[p] for p in range(2)]
    pres += [grads[rows:] * other_slopes[p] for p in range(2)]
    pres = jnp.concatenate([pre.astype(BF16) for pre in pres], axis=0)
    total = mm(jnp.concatenate([left[...], other_left], axis=1), pres)
    quarter = sums.shape[2]
    for j in range(sums.shape[0]):
        sums[j] = total[:, j * quarter : (j + 1) * quarter].astype(BF16)
        stores.append(pltpu.make_async_copy(sums.at[j], sums_out.at[halves[j]], sems.at[1 + j]))
        stores[-1].start()
    settle(stores)


def merge_kernel(bases, offsets, pooled, other, valid, bias, *refs):
    weights, out, whole, sems = refs[:-3], refs[-3], refs[-2], refs[-1]
    count = (len(weights) - 1) // 2
    quarter = whole.shape[1] // (count // 3 + 1)
    loads = []
    for n in range(2):
        start = pl.multiple_of(bases[n], 16)
        loads.append((weights[0].at[pl.ds(start, quarter)], whole.at[n, pl.ds(0, quarter)]))
        for i in range(count):
            ref = weights[1 + n * count + i]
            start = pl.multiple_of(offsets[i], 16)
            loads.append((ref, whole.at[n, pl.ds(start, ref.shape[0])]))
    loads = [
        pltpu.make_async_copy(source, target, sems.at[i]) for i, (source, target) in enumerate(loads)
    ]
    fetch(loads)
    settle(loads)
    total = mm(pooled[...], whole[0]) + mm(other[...], whole[1]) + bias[...]
    out[...] = jnp.where(valid[:, 0:1] > 0.0, total, 0.0).astype(BF16)


def sum_kernel(pieces, out):
    share = pieces.shape[2]
    for core in range(2):
        total = pieces[core].astype(F32)
        for n in range(core + 2, pieces.shape[0], 2):
            total = total + pieces[n].astype(F32)
        out[:, core * share : (core + 1) * share] = total


def body(mel_frames, positions, conv_weight, conv_bias, proj_weight, proj_bias, cotangent):
    recs, owners = lax.axis_size("dp"), lax.axis_size("seq")
    dp_index, seq_index = lax.axis_index("dp"), lax.axis_index("seq")
    core, side = seq_index % 2, (seq_index // 2) % 2
    frames, mel = mel_frames.shape[1:]
    toks = positions.shape[1]
    rows, feats = cotangent.shape[1:]
    capacity = rows // owners
    slots = owners * capacity
    taps = conv_weight.shape[1]
    depth = taps * mel
    chans = proj_weight.shape[0]
    quarter = chans // 2
    width = recs * quarter
    assert taps == 3 and toks == LANES == mel and frames == 2 * toks and rows <= 256

    def shift(x, by):
        return lax.ppermute(x, "dp", [(i, (i + by) % recs) for i in range(recs)])

    def swap(x, bit):
        return lax.ppermute(x, "seq", [(i, i ^ bit) for i in range(owners)])

    end = quarter * 3 // 10 // 16 * 16
    middle = quarter - 2 * end
    base = core * quarter
    head = lax.dynamic_slice_in_dim(proj_weight, base + side * (end + middle), end, 0)
    heads = [shift(head, j) for j in range(1, recs)]
    tails = [swap(h, 2) for h in heads]
    weight_in, _ = lax.optimization_barrier((proj_weight, head))
    mid = lax.dynamic_slice_in_dim(weight_in, base + end, middle, 0)
    mids = [shift(mid, j) for j in range(1, recs)]
    from_here = [(j + 1) * quarter + side * (end + middle) for j in range(recs - 1)]
    from_next = [(j + 1) * quarter + (1 - side) * (end + middle) for j in range(recs - 1)]
    centre = [jnp.asarray((j + 1) * quarter + end, I32) for j in range(recs - 1)]
    early = jnp.stack(from_here).astype(I32)
    late = jnp.stack(centre + from_next).astype(I32)
    offsets = jnp.concatenate([early, late])
    base_in = base.reshape(1).astype(I32)
    bases = jnp.stack([base, (1 - core) * quarter]).astype(I32)
    halves = jnp.stack([(dp_index - j) % recs for j in range(recs)]).astype(I32)
    smem = pl.BlockSpec(memory_space=pltpu.SMEM)
    vmem = pl.BlockSpec(memory_space=pltpu.VMEM)
    hbm = pl.BlockSpec(memory_space=HBM)
    anywhere = pl.BlockSpec(memory_space=pl.ANY)

    cot_own = in_hbm(cotangent[0])
    cot_other = swap(cot_own, 1)

    mel_in, spots_in, _, _ = lax.optimization_barrier((mel_frames[0], positions, head, mid))
    mel_in, spots_in = in_hbm(mel_in), in_hbm(spots_in)
    packed = call(
        functools.partial(pack_kernel, owners, capacity, rows),
        HBM((slots, 4 * mel + LANES), BF16),
        "pack_patches",
        in_specs=[hbm, hbm],
        scratch_shapes=[
            pltpu.VMEM((frames, mel), BF16),
            pltpu.VMEM((1, toks), I32),
            pltpu.SemaphoreType.DMA((2,)),
        ],
    )(mel_in, spots_in)
    arrived = lax.all_to_all(
        packed.reshape(owners, capacity, -1), "seq", split_axis=0, concat_axis=0, tiled=True
    ).reshape(slots, -1)
    def mine(x):
        starts = [(halves[j] * 2 + core) * quarter for j in range(recs)]
        return jnp.concatenate(
            [lax.dynamic_slice_in_dim(x, at, quarter, 1) for at in starts], axis=1
        )

    conv_in, bias_in, _ = lax.optimization_barrier((conv_weight, conv_bias, heads))
    kernel = mine(jnp.transpose(conv_in, (1, 0, 2)).reshape(depth, -1))
    bias = mine(bias_in[None, :])
    share = mel // owners
    arrived, kernel, bias = lax.optimization_barrier((arrived, kernel, bias))
    arrived_other = swap(arrived, 1)
    late_weights = mids + tails

    cots, whole, left, slopes, pooled, valid = call(
        functools.partial(prepare_kernel, share),
        [
            pltpu.VMEM((2 * rows, feats), BF16),
            pltpu.VMEM((width, feats), BF16),
            pltpu.VMEM((depth, 2 * rows), BF16),
            pltpu.VMEM((2, rows, width), F32),
            pltpu.VMEM((rows, width), BF16),
            pltpu.VMEM((rows, LANES), F32),
        ],
        "prepare",
        in_specs=[smem, smem] + [vmem] * 3 + [anywhere] * 3 + [vmem] * len(heads),
        out_specs=[vmem] * 6,
        scratch_shapes=[pltpu.SemaphoreType.DMA((3,))],
    )(base_in, early, arrived, kernel, bias, cot_own, cot_other, in_hbm(proj_weight), *heads)

    sums, pooled_other, _ = call(
        functools.partial(backward_kernel, share),
        [
            HBM((recs, depth, quarter), BF16),
            HBM((rows, width), BF16),
            pltpu.VMEM((width, feats), BF16),
        ],
        "backward",
        in_specs=[smem, smem] + [vmem] * (7 + len(late_weights)),
        out_specs=[hbm, hbm, vmem],
        input_output_aliases={3: 2},
        scratch_shapes=[
            pltpu.VMEM((recs, depth, quarter), BF16),
            pltpu.VMEM((rows, width), BF16),
            pltpu.SemaphoreType.DMA((1 + recs,)),
        ],
    )(late, halves, cots, whole, left, slopes, kernel, bias, arrived_other, *late_weights)
    pieces = lax.all_to_all(
        sums.reshape(recs * owners, taps * share, quarter),
        ("dp", "seq"),
        split_axis=0,
        concat_axis=0,
        tiled=True,
    )
    foreign = heads + late_weights
    merged = call(
        merge_kernel,
        HBM((rows, feats), BF16),
        "merge",
        in_specs=[smem, smem] + [vmem] * 4 + [anywhere] * (1 + 2 * len(foreign)),
        scratch_shapes=[
            pltpu.VMEM((2, width, feats), BF16),
            pltpu.SemaphoreType.DMA((2 + 2 * len(foreign),)),
        ],
    )(
        bases,
        offsets,
        pooled,
        swap(pooled_other, 1),
        valid,
        proj_bias[None, :],
        in_hbm(proj_weight),
        *foreign,
        *[swap(w, 1) for w in foreign],
    )
    pieces, merged = lax.optimization_barrier((pieces, merged))
    grad_weight = call(
        sum_kernel,
        jax.ShapeDtypeStruct((taps * share, chans), F32),
        "sum_pieces",
    )(pieces)
    grad_weight = jnp.transpose(grad_weight.reshape(taps, share, chans), (1, 0, 2))
    return merged[None], grad_weight


def solution(mesh):
    in_specs = (
        P("dp", "seq", None),
        P("dp", "seq"),
        P(),
        P(),
        P("dp", None),
        P(),
        P("dp", "seq", None),
    )
    out_specs = (P("dp", "seq", None), P("seq", None, "dp"))
    return jax.shard_map(body, mesh=mesh, in_specs=in_specs, out_specs=out_specs, check_vma=False)
```

```python
import functools

import jax
import jax.numpy as jnp
from jax import lax
from jax.experimental import pallas as pl
from jax.experimental.pallas import tpu as pltpu
from jax.sharding import PartitionSpec as P

SQRT_HALF = 0.7071067811865476
INV_SQRT_TWO_PI = 0.3989422804014327
LANES = 128
VMEM_LIMIT = 16 * 1024 * 1024
HBM = pltpu.MemorySpace.HBM
F32, BF16, I32 = jnp.float32, jnp.bfloat16, jnp.int32


def iota(shape, dim):
    return lax.broadcasted_iota(I32, shape, dim)


def mm(a, b):
    return jnp.dot(a, b, preferred_element_type=F32)


def call(kernel, out_shape, name, micros=1, **kwargs):
    cost = pl.CostEstimate(flops=micros * 10**9, bytes_accessed=0, transcendentals=0)
    return pl.pallas_call(
        kernel,
        out_shape=out_shape,
        compiler_params=pltpu.CompilerParams(vmem_limit_bytes=VMEM_LIMIT),
        cost_estimate=cost,
        name=name,
        **kwargs,
    )


def in_hbm(x):
    return pltpu.with_memory_space_constraint(x, HBM)


def fetch(copies):
    for copy in copies:
        copy.start()


def settle(copies):
    for copy in copies:
        copy.wait()


def pack_kernel(owners, capacity, rows_own, cuts, mel_hbm, spots_hbm, weight, out, head, far, mel_ref, spots_ref, sems):
    loads = [
        pltpu.make_async_copy(spots_hbm, spots_ref, sems.at[0]),
        pltpu.make_async_copy(mel_hbm, mel_ref, sems.at[1]),
    ]
    fetch(loads)
    unit = head.shape[0]
    rows = []
    targets = [head, far.at[pl.ds(0, unit)]]
    if far.shape[0] > unit:
        targets.append(far.at[pl.ds(unit, far.shape[0] - unit)])
    for n, ref in enumerate(targets):
        start = pl.multiple_of(cuts[n], 16)
        rows.append(
            pltpu.make_async_copy(weight.at[pl.ds(start, ref.shape[0])], ref, sems.at[2 + n])
        )
    fetch(rows)
    high = min(capacity, 8)
    slots = owners * high
    frames, mel = mel_ref.shape
    toks = frames // 2
    before = (iota((toks, toks), 0) < iota((toks, toks), 1)).astype(F32).astype(BF16)
    lane = iota((slots, LANES), 1)
    picks = [
        (iota((toks, frames), 1) == 2 * iota((toks, frames), 0) - 1 + k).astype(F32).astype(BF16)
        for k in range(4)
    ]
    settle(loads)
    spots = spots_ref[...]
    owner = spots // rows_own
    row = (spots - owner * rows_own - rows_own).astype(F32)
    mine = (iota((owners, toks), 0) == owner).astype(F32)
    ahead = mm(mine.astype(BF16), before)
    rank = jnp.sum(mine * ahead, axis=0, keepdims=True).astype(I32)
    window = mel_ref[...]
    patch = jnp.concatenate([mm(pick, window).astype(BF16) for pick in picks], axis=1)
    places = jnp.zeros((slots, LANES), F32)
    width = 4 * mel
    for g in range(capacity // high):
        within = rank - g * high
        target = jnp.where((within >= 0) & (within < high), owner * high + within, -1)
        onehot = (iota((slots, toks), 0) == target).astype(F32)
        spot = jnp.sum(onehot * row, axis=1, keepdims=True) + rows_own
        places = jnp.where(lane == g, spot, places)
        out[:, g * width : (g + 1) * width] = mm(onehot.astype(BF16), patch).astype(BF16)
    out[:, capacity // high * width :] = places.astype(BF16)
    settle(rows)


def rows_from_slots(arrived, rows, mel):
    width = 4 * mel
    groups = arrived.shape[1] // width
    places = jnp.transpose(arrived[:, groups * width :].astype(F32)).astype(I32)
    patch, valid = None, None
    for g in range(groups):
        onehot = (iota((rows, places.shape[1]), 0) == places[g : g + 1, :]).astype(F32)
        part = mm(onehot.astype(BF16), arrived[:, g * width : (g + 1) * width])
        patch = part if patch is None else patch + part
        valid = onehot if valid is None else valid + onehot
    return patch.astype(BF16), valid


LAST = (((1,), (1,)), ((), ()))


def ordered(frames, taps, share):
    depth = frames.shape[1]
    mel = depth // taps
    row = iota((depth, 1), 0).astype(F32)
    block = jnp.floor((row + 0.5) / (taps * share))
    within = row - block * (taps * share)
    tap = jnp.floor((within + 0.5) / share)
    source = (tap * mel + block * share + within - tap * share).astype(I32)
    order = (iota((depth, depth), 1) == source).astype(F32).astype(BF16)
    return lax.dot_general(order, frames, LAST, preferred_element_type=F32).astype(BF16)


def activations(frames, kernel, bias, rows):
    acts = mm(frames, kernel) + bias
    pool, slopes = None, []
    for p in range(2):
        x = acts[p * rows : (p + 1) * rows]
        cdf = 0.5 * (1.0 + lax.erf(x * SQRT_HALF))
        act = x * cdf
        pool = act if pool is None else pool + act
        slopes.append(0.5 * (cdf + x * INV_SQRT_TWO_PI * jnp.exp(-0.5 * x * x)))
    return (0.5 * pool).astype(BF16), slopes


def both_frames(patch, depth):
    mel = patch.shape[1] // 4
    return jnp.concatenate([patch[:, p * mel : p * mel + depth] for p in range(2)], axis=0)


def activate(share, arrived, kernel, bias, left, slopes):
    rows = slopes.shape[1]
    depth = kernel.shape[0]
    patch, found = rows_from_slots(arrived[...], rows, LANES)
    frames = both_frames(patch, depth)
    left[...] = ordered(frames, depth // LANES, share)
    pooled, halves = activations(frames, kernel[...], bias[...], rows)
    for p in range(2):
        slopes[p] = halves[p]
    return pooled, found


def prepare_kernel(share, base, offsets, arrived, kernel, bias, own_in, other_in, weight_in, *refs):
    count = offsets.shape[0]
    heads, refs = refs[:count], refs[count:]
    cots, whole, left, slopes, pooled, valid, *ahead, sems = refs
    rows = pooled.shape[0]
    quarter = whole.shape[0] // (len(heads) + 1)
    start = pl.multiple_of(base[0], 16)
    loads = [
        pltpu.make_async_copy(own_in, cots.at[pl.ds(0, rows)], sems.at[0]),
        pltpu.make_async_copy(
            weight_in.at[pl.ds(start, quarter)], whole.at[pl.ds(0, quarter)], sems.at[1]
        ),
    ]
    fetch(loads)
    place(offsets, heads, whole, len(heads))
    cots[rows:, :] = other_in[...]
    pooled[...], found = activate(share, arrived, kernel, bias, left, slopes)
    valid[...] = jnp.broadcast_to(jnp.sum(found, axis=1, keepdims=True), valid.shape)
    settle(loads)
    if not ahead:
        return
    own_early, other_early = ahead
    early = own_early.shape[1]
    grads = lax.dot_general(cots[...], whole[0:early, :], LAST, preferred_element_type=F32)
    grads = grads.astype(BF16)
    other_early[...] = grads[rows:]
    own_early[...] = mm(left[...], sloped(grads[:rows].astype(F32), slopes[:, :, 0:early]))


def segments(offsets, weights, whole, groups):
    quarter = whole.shape[0] // (groups + 1)
    unit = min(ref.shape[0] for ref in weights)
    out = []
    for n, ref in enumerate(weights):
        start = pl.multiple_of(offsets[n], 16)
        out.append((ref.at[pl.ds(0, unit)], whole.at[pl.ds(start, unit)]))
        if (more := ref.shape[0] - unit) > 0:
            end = (n % groups + 2) * quarter
            out.append((ref.at[pl.ds(unit, more)], whole.at[pl.ds(end - more, more)]))
    return out


def sloped(grads, slopes):
    return jnp.concatenate([(grads * slopes[p]).astype(BF16) for p in range(2)], axis=0)


def place(offsets, weights, whole, groups):
    for source, target in segments(offsets, weights, whole, groups):
        target[...] = source[...]


def backward_kernel(share, early, offsets, halves, cots, whole_in, left, slopes, kernel, bias, arrived, *refs):
    ahead, refs = (refs[:2], refs[2:]) if early else ((), refs)
    weights, refs = refs[:-8], refs[-8:]
    sums_out, pooled_out, whole, sums, pooled, other_left, other_slopes, sems = refs
    rows = cots.shape[0] // 2
    place(offsets, weights, whole, len(weights) // 3)
    pooled[...], _ = activate(share, arrived, kernel, bias, other_left, other_slopes)
    stores = [pltpu.make_async_copy(pooled, pooled_out, sems.at[0])]
    stores[0].start()
    weight = whole[early:, :]
    grads = lax.dot_general(cots[:rows, :], weight, LAST, preferred_element_type=F32)
    grads = grads.astype(BF16).astype(F32)
    own = mm(left[...], sloped(grads, slopes[:, :, early:]))
    grads = lax.dot_general(cots[rows:, :], weight, LAST, preferred_element_type=F32).astype(BF16)
    if ahead:
        own = jnp.concatenate([ahead[0][...], own], axis=1)
        grads = jnp.concatenate([ahead[1][...], grads], axis=1)
    total = own + mm(other_left[...], sloped(grads.astype(F32), other_slopes[...]))
    quarter = total.shape[1] // sums.shape[0]
    for j in range(sums.shape[0]):
        group = total[:, j * quarter : (j + 1) * quarter]
        if sums.shape[-1] > quarter:
            group = group.reshape(sums.shape[1], -1, share, quarter)
            group = jnp.concatenate([group[:, k] for k in range(group.shape[1])], axis=2)
        sums[j] = group.astype(BF16)
        stores.append(pltpu.make_async_copy(sums.at[j], sums_out.at[halves[j]], sems.at[1 + j]))
        stores[-1].start()
    settle(stores)


def merge_kernel(quarter, bases, offsets, pooled, other, valid, bias, *refs):
    weights, out, whole, sems = refs[:-3], refs[-3], refs[-2], refs[-1]
    count = (len(weights) - 1) // 2
    loads = []
    for n in range(2):
        start = pl.multiple_of(bases[n], 16)
        loads.append((weights[0].at[pl.ds(start, quarter)], whole.at[n, pl.ds(0, quarter)]))
        foreign = weights[1 + n * count : 1 + (n + 1) * count]
        loads += segments(offsets, foreign, whole.at[n], count // 4)
    loads = [
        pltpu.make_async_copy(source, target, sems.at[i]) for i, (source, target) in enumerate(loads)
    ]
    fetch(loads)
    settle(loads)
    total = mm(pooled[...], whole[0]) + mm(other[...], whole[1]) + bias[...]
    out[...] = jnp.where(valid[:, 0:1] > 0.0, total, 0.0).astype(BF16)


def sum_kernel(quarter, pieces, out):
    for core in range(2):
        total = pieces[core].astype(F32)
        for n in range(core + 2, pieces.shape[0], 2):
            total = total + pieces[n].astype(F32)
        height = total.shape[0]
        for k in range(total.shape[1] // quarter):
            out[k * height : (k + 1) * height, core * quarter : (core + 1) * quarter] = total[
                :, k * quarter : (k + 1) * quarter
            ]


def body(mel_frames, positions, conv_weight, conv_bias, proj_weight, proj_bias, cotangent):
    recs, owners = lax.axis_size("dp"), lax.axis_size("seq")
    dp_index, seq_index = lax.axis_index("dp"), lax.axis_index("seq")
    core, side = seq_index % 2, (seq_index // 2) % 2
    frames, mel = mel_frames.shape[1:]
    toks = positions.shape[1]
    rows, feats = cotangent.shape[1:]
    capacity = rows // owners
    taps = conv_weight.shape[1]
    depth = taps * mel
    chans = proj_weight.shape[0]
    quarter = chans // 2
    width = recs * quarter
    assert taps == 3 and toks == LANES == mel and frames == 2 * toks and rows <= 256

    def shift(x, by):
        return lax.ppermute(x, "dp", [(i, (i + by) % recs) for i in range(recs)])

    def swap(x, bit):
        return lax.ppermute(x, "seq", [(i, i ^ bit) for i in range(owners)])

    bit = (seq_index // 4) % 2
    unit = quarter // 64 * 16
    base = core * quarter
    part = (bit * 2 + side) * unit
    part_x = (bit * 2 + 1 - side) * unit
    part_z = ((1 - bit) * 2 + side) * unit
    part_far = ((1 - bit) * 2 + 1 - side) * unit
    cuts = jnp.stack([base + part, base + part_far, base + 4 * unit]).astype(I32)
    early = jnp.stack([(j + 1) * quarter + part for j in range(recs - 1)]).astype(I32)
    late = [(j + 1) * quarter + p for p in (part_x, part_z, part_far) for j in range(recs - 1)]
    late = jnp.stack(late).astype(I32)
    offsets = jnp.concatenate([early, late])
    base_in = base.reshape(1).astype(I32)
    bases = jnp.stack([base, (1 - core) * quarter]).astype(I32)
    halves = jnp.stack([(dp_index - j) % recs for j in range(recs)]).astype(I32)
    smem = pl.BlockSpec(memory_space=pltpu.SMEM)
    vmem = pl.BlockSpec(memory_space=pltpu.VMEM)
    hbm = pl.BlockSpec(memory_space=HBM)
    anywhere = pl.BlockSpec(memory_space=pl.ANY)

    high = min(capacity, 8)
    slots = owners * high
    wide_slots = capacity // high * 4 * mel + LANES
    packed, head, far = call(
        functools.partial(pack_kernel, owners, capacity, rows),
        [
            HBM((slots, wide_slots), BF16),
            pltpu.VMEM((unit, feats), BF16),
            pltpu.VMEM((quarter - 3 * unit, feats), BF16),
        ],
        "pack_patches",
        in_specs=[smem, hbm, hbm, hbm],
        out_specs=[vmem] * 3,
        scratch_shapes=[
            pltpu.VMEM((frames, mel), BF16),
            pltpu.VMEM((1, toks), I32),
            pltpu.SemaphoreType.DMA((5,)),
        ],
    )(cuts, in_hbm(mel_frames[0]), in_hbm(positions), in_hbm(proj_weight))
    heads = [shift(head, j) for j in range(1, recs)]
    by_x = [swap(h, 2) for h in heads]
    by_z = [swap(h, 4) for h in heads]
    cot_in, _ = lax.optimization_barrier((cotangent[0], packed))
    late_weights = by_x + by_z + [shift(far, j) for j in range(1, recs)]
    cot_own = in_hbm(cot_in)
    cot_other = swap(cot_in, 1)

    arrived = lax.all_to_all(
        packed.reshape(owners, high, -1), "seq", split_axis=0, concat_axis=0, tiled=True
    ).reshape(slots, -1)
    def mine(x):
        starts = [(halves[j] * 2 + core) * quarter for j in range(recs)]
        return jnp.concatenate(
            [lax.dynamic_slice_in_dim(x, at, quarter, 1) for at in starts], axis=1
        )

    conv_in, bias_in, _ = lax.optimization_barrier((conv_weight, conv_bias, heads))
    kernel = mine(jnp.transpose(conv_in, (1, 0, 2)).reshape(depth, -1))
    bias = mine(bias_in[None, :])
    share = mel // owners
    wide = share % 8 == 0
    packet = (recs, owners, share, taps * quarter) if wide else (recs, depth, quarter)
    arrived, kernel, bias = lax.optimization_barrier((arrived, kernel, bias))
    arrived_other = swap(arrived, 1)

    early_lanes = quarter // LANES * LANES
    cots, whole, left, slopes, pooled, valid, *ahead = call(
        functools.partial(prepare_kernel, share),
        [
            pltpu.VMEM((2 * rows, feats), BF16),
            pltpu.VMEM((width, feats), BF16),
            pltpu.VMEM((depth, 2 * rows), BF16),
            pltpu.VMEM((2, rows, width), F32),
            pltpu.VMEM((rows, width), BF16),
            pltpu.VMEM((rows, LANES), F32),
        ]
        + (
            [pltpu.VMEM((depth, early_lanes), F32), pltpu.VMEM((rows, early_lanes), BF16)]
            if early_lanes
            else []
        ),
        "prepare",
        in_specs=[smem, smem] + [vmem] * 3 + [anywhere, vmem, anywhere] + [vmem] * len(heads),
        out_specs=[vmem] * (8 if early_lanes else 6),
        scratch_shapes=[pltpu.SemaphoreType.DMA((2,))],
    )(base_in, early, arrived, kernel, bias, cot_own, cot_other, in_hbm(proj_weight), *heads)

    sums, pooled_other, _ = call(
        functools.partial(backward_kernel, share, early_lanes),
        [HBM(packet, BF16), HBM((rows, width), BF16), pltpu.VMEM((width, feats), BF16)],
        "backward",
        in_specs=[smem, smem] + [vmem] * (7 + len(ahead) + len(late_weights)),
        out_specs=[hbm, hbm, vmem],
        input_output_aliases={3: 2},
        scratch_shapes=[
            pltpu.VMEM(packet, BF16),
            pltpu.VMEM((rows, width), BF16),
            pltpu.VMEM((depth, 2 * rows), BF16),
            pltpu.VMEM((2, rows, width), F32),
            pltpu.SemaphoreType.DMA((1 + recs,)),
        ],
    )(late, halves, cots, whole, left, slopes, kernel, bias, arrived_other, *ahead, *late_weights)
    pieces = lax.all_to_all(
        sums.reshape((recs * owners, -1, packet[-1])),
        ("dp", "seq"),
        split_axis=0,
        concat_axis=0,
        tiled=True,
    )
    foreign = heads + late_weights
    merged = call(
        functools.partial(merge_kernel, quarter),
        HBM((rows, feats), BF16),
        "merge",
        in_specs=[smem, smem] + [vmem] * 4 + [anywhere] * (1 + 2 * len(foreign)),
        scratch_shapes=[
            pltpu.VMEM((2, width, feats), BF16),
            pltpu.SemaphoreType.DMA((2 + 4 * len(foreign),)),
        ],
    )(
        bases,
        offsets,
        pooled,
        swap(pooled_other, 1),
        valid,
        proj_bias[None, :],
        in_hbm(proj_weight),
        *foreign,
        *[swap(w, 1) for w in foreign],
    )
    pieces, merged = lax.optimization_barrier((pieces, merged))
    grad_weight = call(
        functools.partial(sum_kernel, quarter),
        jax.ShapeDtypeStruct((taps * share, chans), F32),
        "sum_pieces",
    )(pieces)
    grad_weight = jnp.transpose(grad_weight.reshape(taps, share, chans), (1, 0, 2))
    return merged[None], grad_weight


def solution(mesh):
    in_specs = (
        P("dp", "seq", None),
        P("dp", "seq"),
        P(),
        P(),
        P("dp", None),
        P(),
        P("dp", "seq", None),
    )
    out_specs = (P("dp", "seq", None), P("seq", None, "dp"))
    return jax.shard_map(body, mesh=mesh, in_specs=in_specs, out_specs=out_specs, check_vma=False)
```

```python
import functools

import jax
import jax.numpy as jnp
from jax import lax
from jax.experimental import pallas as pl
from jax.experimental.pallas import tpu as pltpu
from jax.sharding import PartitionSpec as P

SQRT_HALF = 0.7071067811865476
INV_SQRT_TWO_PI = 0.3989422804014327
LANES = 128
VMEM_LIMIT = 16 * 1024 * 1024
HBM = pltpu.MemorySpace.HBM
F32, BF16, I32 = jnp.float32, jnp.bfloat16, jnp.int32


def iota(shape, dim):
    return lax.broadcasted_iota(I32, shape, dim)


def mm(a, b):
    return jnp.dot(a, b, preferred_element_type=F32)


def call(kernel, out_shape, name, micros=1, **kwargs):
    cost = pl.CostEstimate(flops=micros * 10**9, bytes_accessed=0, transcendentals=0)
    return pl.pallas_call(
        kernel,
        out_shape=out_shape,
        compiler_params=pltpu.CompilerParams(vmem_limit_bytes=VMEM_LIMIT),
        cost_estimate=cost,
        name=name,
        **kwargs,
    )


def in_hbm(x):
    return pltpu.with_memory_space_constraint(x, HBM)


def fetch(copies):
    for copy in copies:
        copy.start()


def settle(copies):
    for copy in copies:
        copy.wait()


def pack_kernel(owners, capacity, rows_own, cuts, mel_hbm, spots_hbm, weight, out, head, mel_ref, spots_ref, sems):
    loads = [
        pltpu.make_async_copy(spots_hbm, spots_ref, sems.at[0]),
        pltpu.make_async_copy(mel_hbm, mel_ref, sems.at[1]),
    ]
    fetch(loads)
    start = pl.multiple_of(cuts[0], 16)
    rows = pltpu.make_async_copy(weight.at[pl.ds(start, head.shape[0])], head, sems.at[2])
    rows.start()
    high = min(capacity, 8)
    slots = owners * high
    frames, mel = mel_ref.shape
    toks = frames // 2
    before = (iota((toks, toks), 0) < iota((toks, toks), 1)).astype(F32).astype(BF16)
    lane = iota((slots, LANES), 1)
    picks = [
        (iota((toks, frames), 1) == 2 * iota((toks, frames), 0) - 1 + k).astype(F32).astype(BF16)
        for k in range(4)
    ]
    settle(loads)
    spots = spots_ref[...]
    owner = spots // rows_own
    row = (spots - owner * rows_own - rows_own).astype(F32)
    mine = (iota((owners, toks), 0) == owner).astype(F32)
    ahead = mm(mine.astype(BF16), before)
    rank = jnp.sum(mine * ahead, axis=0, keepdims=True).astype(I32)
    window = mel_ref[...]
    patch = jnp.concatenate([mm(pick, window).astype(BF16) for pick in picks], axis=1)
    places = jnp.zeros((slots, LANES), F32)
    width = 4 * mel
    for g in range(capacity // high):
        within = rank - g * high
        target = jnp.where((within >= 0) & (within < high), owner * high + within, -1)
        onehot = (iota((slots, toks), 0) == target).astype(F32)
        spot = jnp.sum(onehot * row, axis=1, keepdims=True) + rows_own
        places = jnp.where(lane == g, spot, places)
        out[:, g * width : (g + 1) * width] = mm(onehot.astype(BF16), patch).astype(BF16)
    out[:, capacity // high * width :] = places.astype(BF16)
    rows.wait()


def rows_from_slots(arrived, rows, mel):
    width = 4 * mel
    groups = arrived.shape[1] // width
    places = jnp.transpose(arrived[:, groups * width :].astype(F32)).astype(I32)
    patch, valid = None, None
    for g in range(groups):
        onehot = (iota((rows, places.shape[1]), 0) == places[g : g + 1, :]).astype(F32)
        part = mm(onehot.astype(BF16), arrived[:, g * width : (g + 1) * width])
        patch = part if patch is None else patch + part
        valid = onehot if valid is None else valid + onehot
    return patch.astype(BF16), valid


LAST = (((1,), (1,)), ((), ()))


def ordered(frames, taps, share):
    depth = frames.shape[1]
    mel = depth // taps
    row = iota((depth, 1), 0).astype(F32)
    block = jnp.floor((row + 0.5) / (taps * share))
    within = row - block * (taps * share)
    tap = jnp.floor((within + 0.5) / share)
    source = (tap * mel + block * share + within - tap * share).astype(I32)
    order = (iota((depth, depth), 1) == source).astype(F32).astype(BF16)
    return lax.dot_general(order, frames, LAST, preferred_element_type=F32).astype(BF16)


def activations(frames, kernel, bias, rows):
    acts = mm(frames, kernel) + bias
    pool, slopes = None, []
    for p in range(2):
        x = acts[p * rows : (p + 1) * rows]
        cdf = 0.5 * (1.0 + lax.erf(x * SQRT_HALF))
        act = x * cdf
        pool = act if pool is None else pool + act
        slopes.append(0.5 * (cdf + x * INV_SQRT_TWO_PI * jnp.exp(-0.5 * x * x)))
    return (0.5 * pool).astype(BF16), slopes


def both_frames(patch, depth):
    mel = patch.shape[1] // 4
    return jnp.concatenate([patch[:, p * mel : p * mel + depth] for p in range(2)], axis=0)


def activate(share, arrived, kernel, bias, left, slopes):
    rows = slopes.shape[1]
    depth = kernel.shape[0]
    patch, found = rows_from_slots(arrived[...], rows, LANES)
    frames = both_frames(patch, depth)
    left[...] = ordered(frames, depth // LANES, share)
    pooled, halves = activations(frames, kernel[...], bias[...], rows)
    for p in range(2):
        slopes[p] = halves[p]
    return pooled, found


def prepare_kernel(share, base, offsets, arrived, kernel, bias, own_in, other_in, weight_in, *refs):
    count = offsets.shape[0]
    heads, refs = refs[:count], refs[count:]
    cots, whole, left, slopes, pooled, valid, *ahead, sems = refs
    rows = pooled.shape[0]
    quarter = whole.shape[0] // (len(heads) + 1)
    start = pl.multiple_of(base[0], 16)
    loads = [
        pltpu.make_async_copy(own_in, cots.at[pl.ds(0, rows)], sems.at[0]),
        pltpu.make_async_copy(
            weight_in.at[pl.ds(start, quarter)], whole.at[pl.ds(0, quarter)], sems.at[1]
        ),
    ]
    fetch(loads)
    place(offsets, heads, whole, len(heads))
    cots[rows:, :] = other_in[...]
    pooled[...], found = activate(share, arrived, kernel, bias, left, slopes)
    valid[...] = jnp.broadcast_to(jnp.sum(found, axis=1, keepdims=True), valid.shape)
    settle(loads)
    if not ahead:
        return
    own_early, other_early = ahead
    early = own_early.shape[1]
    grads = lax.dot_general(cots[...], whole[0:early, :], LAST, preferred_element_type=F32)
    grads = grads.astype(BF16)
    other_early[...] = grads[rows:]
    own_early[...] = mm(left[...], sloped(grads[:rows].astype(F32), slopes[:, :, 0:early]))


def segments(offsets, weights, whole, groups):
    quarter = whole.shape[0] // (groups + 1)
    unit = min(ref.shape[0] for ref in weights)
    out = []
    for n, ref in enumerate(weights):
        start = pl.multiple_of(offsets[n], 16)
        out.append((ref.at[pl.ds(0, unit)], whole.at[pl.ds(start, unit)]))
        if (more := ref.shape[0] - unit) > 0:
            end = (n % groups + 2) * quarter
            out.append((ref.at[pl.ds(unit, more)], whole.at[pl.ds(end - more, more)]))
    return out


def sloped(grads, slopes):
    return jnp.concatenate([(grads * slopes[p]).astype(BF16) for p in range(2)], axis=0)


def place(offsets, weights, whole, groups):
    for source, target in segments(offsets, weights, whole, groups):
        target[...] = source[...]


def backward_kernel(share, early, offsets, halves, cots, whole_in, left, slopes, kernel, bias, arrived, *refs):
    ahead, refs = (refs[:2], refs[2:]) if early else ((), refs)
    weights, refs = refs[:-8], refs[-8:]
    sums_out, pooled_out, whole, sums, pooled, other_left, other_slopes, sems = refs
    rows = cots.shape[0] // 2
    place(offsets, weights, whole, len(weights) // 3)
    pooled[...], _ = activate(share, arrived, kernel, bias, other_left, other_slopes)
    stores = [pltpu.make_async_copy(pooled, pooled_out, sems.at[0])]
    stores[0].start()
    weight = whole[early:, :]
    grads = lax.dot_general(cots[:rows, :], weight, LAST, preferred_element_type=F32)
    grads = grads.astype(BF16).astype(F32)
    own = mm(left[...], sloped(grads, slopes[:, :, early:]))
    grads = lax.dot_general(cots[rows:, :], weight, LAST, preferred_element_type=F32).astype(BF16)
    if ahead:
        own = jnp.concatenate([ahead[0][...], own], axis=1)
        grads = jnp.concatenate([ahead[1][...], grads], axis=1)
    total = own + mm(other_left[...], sloped(grads.astype(F32), other_slopes[...]))
    quarter = total.shape[1] // sums.shape[0]
    for j in range(sums.shape[0]):
        group = total[:, j * quarter : (j + 1) * quarter]
        if sums.shape[-1] > quarter:
            group = group.reshape(sums.shape[1], -1, share, quarter)
            group = jnp.concatenate([group[:, k] for k in range(group.shape[1])], axis=2)
        sums[j] = group.astype(BF16)
        stores.append(pltpu.make_async_copy(sums.at[j], sums_out.at[halves[j]], sems.at[1 + j]))
        stores[-1].start()
    settle(stores)


def merge_kernel(quarter, bases, offsets, pooled, other, valid, bias, *refs):
    weights, out, whole, sems = refs[:-3], refs[-3], refs[-2], refs[-1]
    count = (len(weights) - 1) // 2
    loads = []
    for n in range(2):
        start = pl.multiple_of(bases[n], 16)
        loads.append((weights[0].at[pl.ds(start, quarter)], whole.at[n, pl.ds(0, quarter)]))
        foreign = weights[1 + n * count : 1 + (n + 1) * count]
        loads += segments(offsets, foreign, whole.at[n], count // 4)
    loads = [
        pltpu.make_async_copy(source, target, sems.at[i]) for i, (source, target) in enumerate(loads)
    ]
    fetch(loads)
    settle(loads)
    total = mm(pooled[...], whole[0]) + mm(other[...], whole[1]) + bias[...]
    out[...] = jnp.where(valid[:, 0:1] > 0.0, total, 0.0).astype(BF16)


def sum_kernel(quarter, pieces, out):
    for core in range(2):
        total = pieces[core].astype(F32)
        for n in range(core + 2, pieces.shape[0], 2):
            total = total + pieces[n].astype(F32)
        height = total.shape[0]
        for k in range(total.shape[1] // quarter):
            out[k * height : (k + 1) * height, core * quarter : (core + 1) * quarter] = total[
                :, k * quarter : (k + 1) * quarter
            ]


def body(mel_frames, positions, conv_weight, conv_bias, proj_weight, proj_bias, cotangent):
    recs, owners = lax.axis_size("dp"), lax.axis_size("seq")
    dp_index, seq_index = lax.axis_index("dp"), lax.axis_index("seq")
    core, side = seq_index % 2, (seq_index // 2) % 2
    frames, mel = mel_frames.shape[1:]
    toks = positions.shape[1]
    rows, feats = cotangent.shape[1:]
    capacity = rows // owners
    taps = conv_weight.shape[1]
    depth = taps * mel
    chans = proj_weight.shape[0]
    quarter = chans // 2
    width = recs * quarter
    assert taps == 3 and toks == LANES == mel and frames == 2 * toks and rows <= 256

    def shift(x, by):
        return lax.ppermute(x, "dp", [(i, (i + by) % recs) for i in range(recs)])

    def swap(x, bit):
        return lax.ppermute(x, "seq", [(i, i ^ bit) for i in range(owners)])

    bit = (seq_index // 4) % 2
    unit = quarter // 64 * 16
    base = core * quarter
    part = (bit * 2 + side) * unit
    part_x = (bit * 2 + 1 - side) * unit
    part_z = ((1 - bit) * 2 + side) * unit
    part_far = ((1 - bit) * 2 + 1 - side) * unit
    cuts = (base + part).reshape(1).astype(I32)
    early = jnp.stack([(j + 1) * quarter + part for j in range(recs - 1)]).astype(I32)
    late = [(j + 1) * quarter + p for p in (part_x, part_z, part_far) for j in range(recs - 1)]
    late = jnp.stack(late).astype(I32)
    offsets = jnp.concatenate([early, late])
    base_in = base.reshape(1).astype(I32)
    bases = jnp.stack([base, (1 - core) * quarter]).astype(I32)
    halves = jnp.stack([(dp_index - j) % recs for j in range(recs)]).astype(I32)
    smem = pl.BlockSpec(memory_space=pltpu.SMEM)
    vmem = pl.BlockSpec(memory_space=pltpu.VMEM)
    hbm = pl.BlockSpec(memory_space=HBM)
    anywhere = pl.BlockSpec(memory_space=pl.ANY)

    high = min(capacity, 8)
    slots = owners * high
    wide_slots = capacity // high * 4 * mel + LANES
    packed, head = call(
        functools.partial(pack_kernel, owners, capacity, rows),
        [
            HBM((slots, wide_slots), BF16),
            pltpu.VMEM((unit, feats), BF16),
        ],
        "pack_patches",
        in_specs=[smem, hbm, hbm, hbm],
        out_specs=[vmem] * 2,
        scratch_shapes=[
            pltpu.VMEM((frames, mel), BF16),
            pltpu.VMEM((1, toks), I32),
            pltpu.SemaphoreType.DMA((3,)),
        ],
    )(cuts, in_hbm(mel_frames[0]), in_hbm(positions), in_hbm(proj_weight))
    heads = [shift(head, j) for j in range(1, recs)]
    by_x = [swap(h, 2) for h in heads]
    by_z = [swap(h, 4) for h in heads]
    weight_in, _ = lax.optimization_barrier((proj_weight, packed))
    far = lax.dynamic_slice_in_dim(weight_in, base + part_far, unit, 0)
    if extra := quarter - 4 * unit:
        last = lax.dynamic_slice_in_dim(weight_in, base + 4 * unit, extra, 0)
        far = jnp.concatenate([far, last], axis=0)
    cot_in, _ = lax.optimization_barrier((cotangent[0], packed))
    late_weights = by_x + by_z + [shift(far, j) for j in range(1, recs)]
    cot_own = in_hbm(cot_in)
    cot_other = swap(cot_in, 1)

    arrived = lax.all_to_all(
        packed.reshape(owners, high, -1), "seq", split_axis=0, concat_axis=0, tiled=True
    ).reshape(slots, -1)
    def mine(x):
        starts = [(halves[j] * 2 + core) * quarter for j in range(recs)]
        return jnp.concatenate(
            [lax.dynamic_slice_in_dim(x, at, quarter, 1) for at in starts], axis=1
        )

    conv_in, bias_in, _ = lax.optimization_barrier((conv_weight, conv_bias, heads))
    kernel = mine(jnp.transpose(conv_in, (1, 0, 2)).reshape(depth, -1))
    bias = mine(bias_in[None, :])
    share = mel // owners
    wide = share % 8 == 0
    packet = (recs, owners, share, taps * quarter) if wide else (recs, depth, quarter)
    arrived, kernel, bias = lax.optimization_barrier((arrived, kernel, bias))
    arrived_other = swap(arrived, 1)

    early_lanes = quarter // LANES * LANES
    cots, whole, left, slopes, pooled, valid, *ahead = call(
        functools.partial(prepare_kernel, share),
        [
            pltpu.VMEM((2 * rows, feats), BF16),
            pltpu.VMEM((width, feats), BF16),
            pltpu.VMEM((depth, 2 * rows), BF16),
            pltpu.VMEM((2, rows, width), F32),
            pltpu.VMEM((rows, width), BF16),
            pltpu.VMEM((rows, LANES), F32),
        ]
        + (
            [pltpu.VMEM((depth, early_lanes), F32), pltpu.VMEM((rows, early_lanes), BF16)]
            if early_lanes
            else []
        ),
        "prepare",
        in_specs=[smem, smem] + [vmem] * 3 + [anywhere, vmem, anywhere] + [vmem] * len(heads),
        out_specs=[vmem] * (8 if early_lanes else 6),
        scratch_shapes=[pltpu.SemaphoreType.DMA((2,))],
    )(base_in, early, arrived, kernel, bias, cot_own, cot_other, in_hbm(proj_weight), *heads)

    sums, pooled_other, _ = call(
        functools.partial(backward_kernel, share, early_lanes),
        [HBM(packet, BF16), HBM((rows, width), BF16), pltpu.VMEM((width, feats), BF16)],
        "backward",
        in_specs=[smem, smem] + [vmem] * (7 + len(ahead) + len(late_weights)),
        out_specs=[hbm, hbm, vmem],
        input_output_aliases={3: 2},
        scratch_shapes=[
            pltpu.VMEM(packet, BF16),
            pltpu.VMEM((rows, width), BF16),
            pltpu.VMEM((depth, 2 * rows), BF16),
            pltpu.VMEM((2, rows, width), F32),
            pltpu.SemaphoreType.DMA((1 + recs,)),
        ],
    )(late, halves, cots, whole, left, slopes, kernel, bias, arrived_other, *ahead, *late_weights)
    pieces = lax.all_to_all(
        sums.reshape((recs * owners, -1, packet[-1])),
        ("dp", "seq"),
        split_axis=0,
        concat_axis=0,
        tiled=True,
    )
    foreign = heads + late_weights
    merged = call(
        functools.partial(merge_kernel, quarter),
        HBM((rows, feats), BF16),
        "merge",
        in_specs=[smem, smem] + [vmem] * 4 + [anywhere] * (1 + 2 * len(foreign)),
        scratch_shapes=[
            pltpu.VMEM((2, width, feats), BF16),
            pltpu.SemaphoreType.DMA((2 + 4 * len(foreign),)),
        ],
    )(
        bases,
        offsets,
        pooled,
        swap(pooled_other, 1),
        valid,
        proj_bias[None, :],
        in_hbm(proj_weight),
        *foreign,
        *[swap(w, 1) for w in foreign],
    )
    pieces, merged = lax.optimization_barrier((pieces, merged))
    grad_weight = call(
        functools.partial(sum_kernel, quarter),
        jax.ShapeDtypeStruct((taps * share, chans), F32),
        "sum_pieces",
    )(pieces)
    grad_weight = jnp.transpose(grad_weight.reshape(taps, share, chans), (1, 0, 2))
    return merged[None], grad_weight


def solution(mesh):
    in_specs = (
        P("dp", "seq", None),
        P("dp", "seq"),
        P(),
        P(),
        P("dp", None),
        P(),
        P("dp", "seq", None),
    )
    out_specs = (P("dp", "seq", None), P("seq", None, "dp"))
    return jax.shard_map(body, mesh=mesh, in_specs=in_specs, out_specs=out_specs, check_vma=False)
```

```python
import functools

import jax
import jax.numpy as jnp
from jax import lax
from jax.experimental import pallas as pl
from jax.experimental.pallas import tpu as pltpu
from jax.sharding import PartitionSpec as P

SQRT_HALF = 0.7071067811865476
INV_SQRT_TWO_PI = 0.3989422804014327
LANES = 128
VMEM_LIMIT = 16 * 1024 * 1024
HBM = pltpu.MemorySpace.HBM
F32, BF16, I32 = jnp.float32, jnp.bfloat16, jnp.int32


def iota(shape, dim):
    return lax.broadcasted_iota(I32, shape, dim)


def mm(a, b):
    return jnp.dot(a, b, preferred_element_type=F32)


def call(kernel, out_shape, name, micros=1, **kwargs):
    cost = pl.CostEstimate(flops=micros * 10**9, bytes_accessed=0, transcendentals=0)
    return pl.pallas_call(
        kernel,
        out_shape=out_shape,
        compiler_params=pltpu.CompilerParams(vmem_limit_bytes=VMEM_LIMIT),
        cost_estimate=cost,
        name=name,
        **kwargs,
    )


def in_hbm(x):
    return pltpu.with_memory_space_constraint(x, HBM)


def fetch(copies):
    for copy in copies:
        copy.start()


def settle(copies):
    for copy in copies:
        copy.wait()


def pack_kernel(owners, capacity, rows_own, cuts, mel_hbm, spots_hbm, weight, out, head, mel_ref, spots_ref, sems):
    loads = [
        pltpu.make_async_copy(spots_hbm, spots_ref, sems.at[0]),
        pltpu.make_async_copy(mel_hbm, mel_ref, sems.at[1]),
    ]
    fetch(loads)
    start = pl.multiple_of(cuts[0], 16)
    rows = pltpu.make_async_copy(weight.at[pl.ds(start, head.shape[0])], head, sems.at[2])
    rows.start()
    high = min(capacity, 8)
    slots = owners * high
    frames, mel = mel_ref.shape
    toks = frames // 2
    before = (iota((toks, toks), 0) < iota((toks, toks), 1)).astype(F32).astype(BF16)
    lane = iota((slots, LANES), 1)
    picks = [
        (iota((toks, frames), 1) == 2 * iota((toks, frames), 0) - 1 + k).astype(F32).astype(BF16)
        for k in range(4)
    ]
    settle(loads)
    spots = spots_ref[...]
    owner = spots // rows_own
    row = (spots - owner * rows_own - rows_own).astype(F32)
    mine = (iota((owners, toks), 0) == owner).astype(F32)
    ahead = mm(mine.astype(BF16), before)
    rank = jnp.sum(mine * ahead, axis=0, keepdims=True).astype(I32)
    window = mel_ref[...]
    patch = jnp.concatenate([mm(pick, window).astype(BF16) for pick in picks], axis=1)
    places = jnp.zeros((slots, LANES), F32)
    width = 4 * mel
    for g in range(capacity // high):
        within = rank - g * high
        target = jnp.where((within >= 0) & (within < high), owner * high + within, -1)
        onehot = (iota((slots, toks), 0) == target).astype(F32)
        spot = jnp.sum(onehot * row, axis=1, keepdims=True) + rows_own
        places = jnp.where(lane == g, spot, places)
        out[:, g * width : (g + 1) * width] = mm(onehot.astype(BF16), patch).astype(BF16)
    out[:, capacity // high * width :] = places.astype(BF16)
    rows.wait()


def rows_from_slots(arrived, rows, mel):
    width = 4 * mel
    groups = arrived.shape[1] // width
    places = jnp.transpose(arrived[:, groups * width :].astype(F32)).astype(I32)
    patch, valid = None, None
    for g in range(groups):
        onehot = (iota((rows, places.shape[1]), 0) == places[g : g + 1, :]).astype(F32)
        part = mm(onehot.astype(BF16), arrived[:, g * width : (g + 1) * width])
        patch = part if patch is None else patch + part
        valid = onehot if valid is None else valid + onehot
    return patch.astype(BF16), valid


LAST = (((1,), (1,)), ((), ()))


def ordered(frames, taps, share):
    depth = frames.shape[1]
    mel = depth // taps
    row = iota((depth, 1), 0).astype(F32)
    block = jnp.floor((row + 0.5) / (taps * share))
    within = row - block * (taps * share)
    tap = jnp.floor((within + 0.5) / share)
    source = (tap * mel + block * share + within - tap * share).astype(I32)
    order = (iota((depth, depth), 1) == source).astype(F32).astype(BF16)
    return lax.dot_general(order, frames, LAST, preferred_element_type=F32).astype(BF16)


def activations(frames, kernel, bias, rows):
    acts = mm(frames, kernel) + bias
    pool, slopes = None, []
    for p in range(2):
        x = acts[p * rows : (p + 1) * rows]
        cdf = 0.5 * (1.0 + lax.erf(x * SQRT_HALF))
        act = x * cdf
        pool = act if pool is None else pool + act
        slopes.append(0.5 * (cdf + x * INV_SQRT_TWO_PI * jnp.exp(-0.5 * x * x)))
    return (0.5 * pool).astype(BF16), slopes


def both_frames(patch, depth):
    mel = patch.shape[1] // 4
    return jnp.concatenate([patch[:, p * mel : p * mel + depth] for p in range(2)], axis=0)


def activate(share, arrived, kernel, bias, left, slopes):
    rows = slopes.shape[1]
    depth = kernel.shape[0]
    patch, found = rows_from_slots(arrived[...], rows, LANES)
    frames = both_frames(patch, depth)
    left[...] = ordered(frames, depth // LANES, share)
    pooled, halves = activations(frames, kernel[...], bias[...], rows)
    for p in range(2):
        slopes[p] = halves[p]
    return pooled, found


def prepare_kernel(share, base, offsets, arrived, kernel, bias, own_in, other_in, weight_in, *refs):
    count = offsets.shape[0]
    heads, refs = refs[:count], refs[count:]
    cots, whole, left, slopes, pooled, valid, *ahead, sems = refs
    rows = pooled.shape[0]
    quarter = whole.shape[0] // (len(heads) + 1)
    start = pl.multiple_of(base[0], 16)
    loads = [
        pltpu.make_async_copy(own_in, cots.at[pl.ds(0, rows)], sems.at[0]),
        pltpu.make_async_copy(
            weight_in.at[pl.ds(start, quarter)], whole.at[pl.ds(0, quarter)], sems.at[1]
        ),
    ]
    fetch(loads)
    place(offsets, heads, whole, len(heads), quarter)
    cots[rows:, :] = other_in[...]
    pooled[...], found = activate(share, arrived, kernel, bias, left, slopes)
    valid[...] = jnp.broadcast_to(jnp.sum(found, axis=1, keepdims=True), valid.shape)
    settle(loads)
    if not ahead:
        return
    own_early, other_early = ahead
    early = own_early.shape[1]
    grads = lax.dot_general(cots[...], whole[0:early, :], LAST, preferred_element_type=F32)
    grads = grads.astype(BF16)
    other_early[...] = grads[rows:]
    own_early[...] = mm(left[...], sloped(grads[:rows].astype(F32), slopes[:, :, 0:early]))


def sloped(grads, slopes):
    return jnp.concatenate([(grads * slopes[p]).astype(BF16) for p in range(2)], axis=0)


def segments(offsets, weights, whole, groups, quarter, skip=0):
    unit = min(ref.shape[0] for ref in weights)
    out = []
    for n, ref in enumerate(weights):
        start = pl.multiple_of(offsets[n] - skip, 16)
        out.append((ref.at[pl.ds(0, unit)], whole.at[pl.ds(start, unit)]))
        if (more := ref.shape[0] - unit) > 0:
            end = (n % groups + 2) * quarter - skip
            out.append((ref.at[pl.ds(unit, more)], whole.at[pl.ds(end - more, more)]))
    return out


def place(*args):
    for source, target in segments(*args):
        target[...] = source[...]


def backward_kernel(share, early, offsets, halves, cots, whole_in, left, slopes, kernel, bias, arrived, *refs):
    ahead, refs = (refs[:2], refs[2:]) if early else ((), refs)
    weights, refs = refs[:-8], refs[-8:]
    sums_out, pooled_out, whole, sums, pooled, other_left, other_slopes, sems = refs
    groups = len(weights) // 3
    rows = cots.shape[0] // 2
    whole[...] = whole_in[early:, :]
    place(offsets, weights, whole, groups, whole_in.shape[0] // (groups + 1), early)
    pooled[...], _ = activate(share, arrived, kernel, bias, other_left, other_slopes)
    stores = [pltpu.make_async_copy(pooled, pooled_out, sems.at[0])]
    stores[0].start()
    weight = whole[...]
    grads = lax.dot_general(cots[:rows, :], weight, LAST, preferred_element_type=F32)
    grads = grads.astype(BF16).astype(F32)
    own = mm(left[...], sloped(grads, slopes[:, :, early:]))
    grads = lax.dot_general(cots[rows:, :], weight, LAST, preferred_element_type=F32).astype(BF16)
    if ahead:
        own = jnp.concatenate([ahead[0][...], own], axis=1)
        grads = jnp.concatenate([ahead[1][...], grads], axis=1)
    total = own + mm(other_left[...], sloped(grads.astype(F32), other_slopes[...]))
    quarter = total.shape[1] // sums.shape[0]
    for j in range(sums.shape[0]):
        group = total[:, j * quarter : (j + 1) * quarter]
        if sums.shape[-1] > quarter:
            group = group.reshape(sums.shape[1], -1, share, quarter)
            group = jnp.concatenate([group[:, k] for k in range(group.shape[1])], axis=2)
        sums[j] = group.astype(BF16)
        stores.append(pltpu.make_async_copy(sums.at[j], sums_out.at[halves[j]], sems.at[1 + j]))
        stores[-1].start()
    settle(stores)


def merge_kernel(quarter, bases, offsets, pooled, other, valid, bias, *refs):
    weights, out, whole, sems = refs[:-3], refs[-3], refs[-2], refs[-1]
    count = (len(weights) - 1) // 2
    loads = []
    for n in range(2):
        start = pl.multiple_of(bases[n], 16)
        loads.append((weights[0].at[pl.ds(start, quarter)], whole.at[n, pl.ds(0, quarter)]))
        foreign = weights[1 + n * count : 1 + (n + 1) * count]
        loads += segments(offsets, foreign, whole.at[n], count // 4, quarter)
    loads = [
        pltpu.make_async_copy(source, target, sems.at[i]) for i, (source, target) in enumerate(loads)
    ]
    fetch(loads)
    settle(loads)
    total = mm(pooled[...], whole[0]) + mm(other[...], whole[1]) + bias[...]
    out[...] = jnp.where(valid[:, 0:1] > 0.0, total, 0.0).astype(BF16)


def sum_kernel(quarter, pieces, out):
    for core in range(2):
        total = pieces[core].astype(F32)
        for n in range(core + 2, pieces.shape[0], 2):
            total = total + pieces[n].astype(F32)
        height = total.shape[0]
        for k in range(total.shape[1] // quarter):
            out[k * height : (k + 1) * height, core * quarter : (core + 1) * quarter] = total[
                :, k * quarter : (k + 1) * quarter
            ]


def body(mel_frames, positions, conv_weight, conv_bias, proj_weight, proj_bias, cotangent):
    recs, owners = lax.axis_size("dp"), lax.axis_size("seq")
    dp_index, seq_index = lax.axis_index("dp"), lax.axis_index("seq")
    core, side = seq_index % 2, (seq_index // 2) % 2
    frames, mel = mel_frames.shape[1:]
    toks = positions.shape[1]
    rows, feats = cotangent.shape[1:]
    capacity = rows // owners
    taps = conv_weight.shape[1]
    depth = taps * mel
    chans = proj_weight.shape[0]
    quarter = chans // 2
    width = recs * quarter
    assert taps == 3 and toks == LANES == mel and frames == 2 * toks and rows <= 256

    def shift(x, by):
        return lax.ppermute(x, "dp", [(i, (i + by) % recs) for i in range(recs)])

    def swap(x, bit):
        return lax.ppermute(x, "seq", [(i, i ^ bit) for i in range(owners)])

    bit = (seq_index // 4) % 2
    unit = quarter // 64 * 16
    base = core * quarter
    part = (bit * 2 + side) * unit
    part_x = (bit * 2 + 1 - side) * unit
    part_z = ((1 - bit) * 2 + side) * unit
    part_far = ((1 - bit) * 2 + 1 - side) * unit
    cuts = (base + part).reshape(1).astype(I32)
    early = jnp.stack([(j + 1) * quarter + part for j in range(recs - 1)]).astype(I32)
    late = [(j + 1) * quarter + p for p in (part_x, part_z, part_far) for j in range(recs - 1)]
    late = jnp.stack(late).astype(I32)
    offsets = jnp.concatenate([early, late])
    base_in = base.reshape(1).astype(I32)
    bases = jnp.stack([base, (1 - core) * quarter]).astype(I32)
    halves = jnp.stack([(dp_index - j) % recs for j in range(recs)]).astype(I32)
    smem = pl.BlockSpec(memory_space=pltpu.SMEM)
    vmem = pl.BlockSpec(memory_space=pltpu.VMEM)
    hbm = pl.BlockSpec(memory_space=HBM)
    anywhere = pl.BlockSpec(memory_space=pl.ANY)

    high = min(capacity, 8)
    slots = owners * high
    wide_slots = capacity // high * 4 * mel + LANES
    packed, head = call(
        functools.partial(pack_kernel, owners, capacity, rows),
        [
            HBM((slots, wide_slots), BF16),
            pltpu.VMEM((unit, feats), BF16),
        ],
        "pack_patches",
        in_specs=[smem, hbm, hbm, hbm],
        out_specs=[vmem] * 2,
        scratch_shapes=[
            pltpu.VMEM((frames, mel), BF16),
            pltpu.VMEM((1, toks), I32),
            pltpu.SemaphoreType.DMA((3,)),
        ],
    )(cuts, in_hbm(mel_frames[0]), in_hbm(positions), in_hbm(proj_weight))
    heads = [shift(head, j) for j in range(1, recs)]
    by_x = [swap(h, 2) for h in heads]
    by_z = [swap(h, 4) for h in heads]
    weight_in, _ = lax.optimization_barrier((proj_weight, packed))
    far = lax.dynamic_slice_in_dim(weight_in, base + part_far, unit, 0)
    if extra := quarter - 4 * unit:
        last = lax.dynamic_slice_in_dim(weight_in, base + 4 * unit, extra, 0)
        far = jnp.concatenate([far, last], axis=0)
    cot_in, _ = lax.optimization_barrier((cotangent[0], packed))
    late_weights = by_x + by_z + [shift(far, j) for j in range(1, recs)]
    cot_own = in_hbm(cot_in)
    cot_other = swap(cot_in, 1)

    arrived = lax.all_to_all(
        packed.reshape(owners, high, -1), "seq", split_axis=0, concat_axis=0, tiled=True
    ).reshape(slots, -1)
    def mine(x):
        starts = [(halves[j] * 2 + core) * quarter for j in range(recs)]
        return jnp.concatenate(
            [lax.dynamic_slice_in_dim(x, at, quarter, 1) for at in starts], axis=1
        )

    conv_in, bias_in, _ = lax.optimization_barrier((conv_weight, conv_bias, heads))
    kernel = mine(jnp.transpose(conv_in, (1, 0, 2)).reshape(depth, -1))
    bias = mine(bias_in[None, :])
    share = mel // owners
    wide = share % 8 == 0
    packet = (recs, owners, share, taps * quarter) if wide else (recs, depth, quarter)
    arrived, kernel, bias = lax.optimization_barrier((arrived, kernel, bias))
    arrived_other = swap(arrived, 1)

    early_lanes = quarter // LANES * LANES
    cots, whole, left, slopes, pooled, valid, *ahead = call(
        functools.partial(prepare_kernel, share),
        [
            pltpu.VMEM((2 * rows, feats), BF16),
            pltpu.VMEM((width, feats), BF16),
            pltpu.VMEM((depth, 2 * rows), BF16),
            pltpu.VMEM((2, rows, width), F32),
            pltpu.VMEM((rows, width), BF16),
            pltpu.VMEM((rows, LANES), F32),
        ]
        + (
            [pltpu.VMEM((depth, early_lanes), F32), pltpu.VMEM((rows, early_lanes), BF16)]
            if early_lanes
            else []
        ),
        "prepare",
        in_specs=[smem, smem] + [vmem] * 3 + [anywhere, vmem, anywhere] + [vmem] * len(heads),
        out_specs=[vmem] * (8 if early_lanes else 6),
        scratch_shapes=[pltpu.SemaphoreType.DMA((2,))],
    )(base_in, early, arrived, kernel, bias, cot_own, cot_other, in_hbm(proj_weight), *heads)

    sums, pooled_other = call(
        functools.partial(backward_kernel, share, early_lanes),
        [HBM(packet, BF16), HBM((rows, width), BF16)],
        "backward",
        in_specs=[smem, smem] + [vmem] * (7 + len(ahead) + len(late_weights)),
        out_specs=[hbm, hbm],
        scratch_shapes=[
            pltpu.VMEM((width - early_lanes, feats), BF16),
            pltpu.VMEM(packet, BF16),
            pltpu.VMEM((rows, width), BF16),
            pltpu.VMEM((depth, 2 * rows), BF16),
            pltpu.VMEM((2, rows, width), F32),
            pltpu.SemaphoreType.DMA((1 + recs,)),
        ],
    )(late, halves, cots, whole, left, slopes, kernel, bias, arrived_other, *ahead, *late_weights)
    pieces = lax.all_to_all(
        sums.reshape((recs * owners, -1, packet[-1])),
        ("dp", "seq"),
        split_axis=0,
        concat_axis=0,
        tiled=True,
    )
    foreign = heads + late_weights
    merged = call(
        functools.partial(merge_kernel, quarter),
        HBM((rows, feats), BF16),
        "merge",
        in_specs=[smem, smem] + [vmem] * 4 + [anywhere] * (1 + 2 * len(foreign)),
        scratch_shapes=[
            pltpu.VMEM((2, width, feats), BF16),
            pltpu.SemaphoreType.DMA((2 + 4 * len(foreign),)),
        ],
    )(
        bases,
        offsets,
        pooled,
        swap(pooled_other, 1),
        valid,
        proj_bias[None, :],
        in_hbm(proj_weight),
        *foreign,
        *[swap(w, 1) for w in foreign],
    )
    pieces, merged = lax.optimization_barrier((pieces, merged))
    grad_weight = call(
        functools.partial(sum_kernel, quarter),
        jax.ShapeDtypeStruct((taps * share, chans), F32),
        "sum_pieces",
    )(pieces)
    grad_weight = jnp.transpose(grad_weight.reshape(taps, share, chans), (1, 0, 2))
    return merged[None], grad_weight


def solution(mesh):
    in_specs = (
        P("dp", "seq", None),
        P("dp", "seq"),
        P(),
        P(),
        P("dp", None),
        P(),
        P("dp", "seq", None),
    )
    out_specs = (P("dp", "seq", None), P("seq", None, "dp"))
    return jax.shard_map(body, mesh=mesh, in_specs=in_specs, out_specs=out_specs, check_vma=False)
```

```python
import functools

import jax
import jax.numpy as jnp
from jax import lax
from jax.experimental import pallas as pl
from jax.experimental.pallas import tpu as pltpu
from jax.sharding import PartitionSpec as P

SQRT_HALF = 0.7071067811865476
INV_SQRT_TWO_PI = 0.3989422804014327
LANES = 128
VMEM_LIMIT = 16 * 1024 * 1024
HBM = pltpu.MemorySpace.HBM
F32, BF16, I32 = jnp.float32, jnp.bfloat16, jnp.int32


def iota(shape, dim):
    return lax.broadcasted_iota(I32, shape, dim)


def mm(a, b):
    return jnp.dot(a, b, preferred_element_type=F32)


def call(kernel, out_shape, name, micros=1, **kwargs):
    cost = pl.CostEstimate(flops=micros * 10**9, bytes_accessed=0, transcendentals=0)
    return pl.pallas_call(
        kernel,
        out_shape=out_shape,
        compiler_params=pltpu.CompilerParams(vmem_limit_bytes=VMEM_LIMIT),
        cost_estimate=cost,
        name=name,
        **kwargs,
    )


def in_hbm(x):
    return pltpu.with_memory_space_constraint(x, HBM)


def fetch(copies):
    for copy in copies:
        copy.start()


def settle(copies):
    for copy in copies:
        copy.wait()


def pack_kernel(owners, capacity, rows_own, cuts, mel_hbm, spots_hbm, weight, out_hbm, head, out, mel_ref, spots_ref, sems):
    loads = [
        pltpu.make_async_copy(spots_hbm, spots_ref, sems.at[0]),
        pltpu.make_async_copy(mel_hbm, mel_ref, sems.at[1]),
    ]
    fetch(loads)
    start = pl.multiple_of(cuts[0], 16)
    rows = pltpu.make_async_copy(weight.at[pl.ds(start, head.shape[0])], head, sems.at[2])
    rows.start()
    high = min(capacity, 8)
    slots = owners * high
    frames, mel = mel_ref.shape
    toks = frames // 2
    before = (iota((toks, toks), 0) < iota((toks, toks), 1)).astype(F32).astype(BF16)
    lane = iota((slots, LANES), 1)
    picks = [
        (iota((toks, frames), 1) == 2 * iota((toks, frames), 0) - 1 + k).astype(F32).astype(BF16)
        for k in range(4)
    ]
    settle(loads)
    spots = spots_ref[...]
    owner = spots // rows_own
    row = (spots - owner * rows_own - rows_own).astype(F32)
    mine = (iota((owners, toks), 0) == owner).astype(F32)
    ahead = mm(mine.astype(BF16), before)
    rank = jnp.sum(mine * ahead, axis=0, keepdims=True).astype(I32)
    window = mel_ref[...]
    patch = jnp.concatenate([mm(pick, window).astype(BF16) for pick in picks], axis=1)
    places = jnp.zeros((slots, LANES), F32)
    width = 4 * mel
    for g in range(capacity // high):
        within = rank - g * high
        target = jnp.where((within >= 0) & (within < high), owner * high + within, -1)
        onehot = (iota((slots, toks), 0) == target).astype(F32)
        spot = jnp.sum(onehot * row, axis=1, keepdims=True) + rows_own
        places = jnp.where(lane == g, spot, places)
        out[:, g * width : (g + 1) * width] = mm(onehot.astype(BF16), patch).astype(BF16)
    out[:, capacity // high * width :] = places.astype(BF16)
    store = pltpu.make_async_copy(out, out_hbm, sems.at[3])
    store.start()
    rows.wait()
    store.wait()


def rows_from_slots(arrived, rows, mel):
    width = 4 * mel
    groups = arrived.shape[1] // width
    places = jnp.transpose(arrived[:, groups * width :].astype(F32)).astype(I32)
    patch, valid = None, None
    for g in range(groups):
        onehot = (iota((rows, places.shape[1]), 0) == places[g : g + 1, :]).astype(F32)
        part = mm(onehot.astype(BF16), arrived[:, g * width : (g + 1) * width])
        patch = part if patch is None else patch + part
        valid = onehot if valid is None else valid + onehot
    return patch.astype(BF16), valid


LAST = (((1,), (1,)), ((), ()))


def ordered(frames, taps, share):
    depth = frames.shape[1]
    mel = depth // taps
    row = iota((depth, 1), 0).astype(F32)
    block = jnp.floor((row + 0.5) / (taps * share))
    within = row - block * (taps * share)
    tap = jnp.floor((within + 0.5) / share)
    source = (tap * mel + block * share + within - tap * share).astype(I32)
    order = (iota((depth, depth), 1) == source).astype(F32).astype(BF16)
    return lax.dot_general(order, frames, LAST, preferred_element_type=F32).astype(BF16)


def activations(frames, kernel, bias, rows):
    acts = mm(frames, kernel) + bias
    pool, slopes = None, []
    for p in range(2):
        x = acts[p * rows : (p + 1) * rows]
        cdf = 0.5 * (1.0 + lax.erf(x * SQRT_HALF))
        act = x * cdf
        pool = act if pool is None else pool + act
        slopes.append(0.5 * (cdf + x * INV_SQRT_TWO_PI * jnp.exp(-0.5 * x * x)))
    return (0.5 * pool).astype(BF16), slopes


def both_frames(patch, depth):
    mel = patch.shape[1] // 4
    return jnp.concatenate([patch[:, p * mel : p * mel + depth] for p in range(2)], axis=0)


def activate(share, arrived, kernel, bias, left, slopes):
    rows = slopes.shape[1]
    depth = kernel.shape[0]
    patch, found = rows_from_slots(arrived[...], rows, LANES)
    frames = both_frames(patch, depth)
    left[...] = ordered(frames, depth // LANES, share)
    pooled, halves = activations(frames, kernel[...], bias[...], rows)
    for p in range(2):
        slopes[p] = halves[p]
    return pooled, found


def prepare_kernel(share, base, offsets, arrived, kernel, bias, own_in, other_in, weight_in, *refs):
    count = offsets.shape[0]
    heads, refs = refs[:count], refs[count:]
    cots, whole, left, slopes, pooled, valid, *ahead, sems = refs
    rows = pooled.shape[0]
    quarter = whole.shape[0] // (len(heads) + 1)
    start = pl.multiple_of(base[0], 16)
    loads = [
        pltpu.make_async_copy(own_in, cots.at[pl.ds(0, rows)], sems.at[0]),
        pltpu.make_async_copy(
            weight_in.at[pl.ds(start, quarter)], whole.at[pl.ds(0, quarter)], sems.at[1]
        ),
    ]
    fetch(loads)
    place(offsets, heads, whole, len(heads), quarter)
    cots[rows:, :] = other_in[...]
    pooled[...], found = activate(share, arrived, kernel, bias, left, slopes)
    valid[...] = jnp.broadcast_to(jnp.sum(found, axis=1, keepdims=True), valid.shape)
    settle(loads)
    if not ahead:
        return
    own_early, other_early = ahead
    early = own_early.shape[1]
    for n in range(2):
        cot = cots[n * rows : (n + 1) * rows, :]
        grads = lax.dot_general(cot, whole[0:early, :], LAST, preferred_element_type=F32)
        grads = grads.astype(BF16)
        if n:
            other_early[...] = grads
        else:
            own_early[...] = mm(left[...], sloped(grads.astype(F32), slopes[:, :, 0:early]))


def sloped(grads, slopes):
    return jnp.concatenate([(grads * slopes[p]).astype(BF16) for p in range(2)], axis=0)


def segments(offsets, weights, whole, groups, quarter, skip=0):
    unit = min(ref.shape[0] for ref in weights)
    out = []
    for n, ref in enumerate(weights):
        start = pl.multiple_of(offsets[n] - skip, 16)
        out.append((ref.at[pl.ds(0, unit)], whole.at[pl.ds(start, unit)]))
        if (more := ref.shape[0] - unit) > 0:
            end = (n % groups + 2) * quarter - skip
            out.append((ref.at[pl.ds(unit, more)], whole.at[pl.ds(end - more, more)]))
    return out


def place(*args):
    for source, target in segments(*args):
        target[...] = source[...]


def backward_kernel(share, early, offsets, halves, cots, whole_in, left, slopes, kernel, bias, arrived, *refs):
    ahead, refs = (refs[:2], refs[2:]) if early else ((), refs)
    weights, refs = refs[:-8], refs[-8:]
    sums_out, pooled_out, whole, sums, pooled, other_left, other_slopes, sems = refs
    groups = len(weights) // 3
    rows = cots.shape[0] // 2
    whole[...] = whole_in[early:, :]
    place(offsets, weights, whole, groups, whole_in.shape[0] // (groups + 1), early)
    pooled[...], _ = activate(share, arrived, kernel, bias, other_left, other_slopes)
    stores = [pltpu.make_async_copy(pooled, pooled_out, sems.at[0])]
    stores[0].start()
    weight = whole[...]
    grads = lax.dot_general(cots[:rows, :], weight, LAST, preferred_element_type=F32)
    grads = grads.astype(BF16).astype(F32)
    own = mm(left[...], sloped(grads, slopes[:, :, early:]))
    grads = lax.dot_general(cots[rows:, :], weight, LAST, preferred_element_type=F32).astype(BF16)
    if ahead:
        own = jnp.concatenate([ahead[0][...], own], axis=1)
        grads = jnp.concatenate([ahead[1][...], grads], axis=1)
    total = own + mm(other_left[...], sloped(grads.astype(F32), other_slopes[...]))
    quarter = total.shape[1] // sums.shape[0]
    for j in range(sums.shape[0]):
        group = total[:, j * quarter : (j + 1) * quarter]
        if sums.shape[-1] > quarter:
            group = group.reshape(sums.shape[1], -1, share, quarter)
            group = jnp.concatenate([group[:, k] for k in range(group.shape[1])], axis=2)
        sums[j] = group.astype(BF16)
        stores.append(pltpu.make_async_copy(sums.at[j], sums_out.at[halves[j]], sems.at[1 + j]))
        stores[-1].start()
    settle(stores)


def merge_kernel(quarter, bases, offsets, pooled, other, valid, bias, *refs):
    weights, out, whole, sems = refs[:-3], refs[-3], refs[-2], refs[-1]
    count = (len(weights) - 1) // 2
    loads = []
    for n in range(2):
        start = pl.multiple_of(bases[n], 16)
        loads.append((weights[0].at[pl.ds(start, quarter)], whole.at[n, pl.ds(0, quarter)]))
        foreign = weights[1 + n * count : 1 + (n + 1) * count]
        loads += segments(offsets, foreign, whole.at[n], count // 4, quarter)
    loads = [
        pltpu.make_async_copy(source, target, sems.at[i]) for i, (source, target) in enumerate(loads)
    ]
    fetch(loads)
    settle(loads)
    total = mm(pooled[...], whole[0]) + mm(other[...], whole[1]) + bias[...]
    out[...] = jnp.where(valid[:, 0:1] > 0.0, total, 0.0).astype(BF16)


def sum_kernel(quarter, pieces, out):
    for core in range(2):
        total = pieces[core].astype(F32)
        for n in range(core + 2, pieces.shape[0], 2):
            total = total + pieces[n].astype(F32)
        height = total.shape[0]
        for k in range(total.shape[1] // quarter):
            out[k * height : (k + 1) * height, core * quarter : (core + 1) * quarter] = total[
                :, k * quarter : (k + 1) * quarter
            ]


def body(mel_frames, positions, conv_weight, conv_bias, proj_weight, proj_bias, cotangent):
    recs, owners = lax.axis_size("dp"), lax.axis_size("seq")
    dp_index, seq_index = lax.axis_index("dp"), lax.axis_index("seq")
    core, side = seq_index % 2, (seq_index // 4) % 2
    frames, mel = mel_frames.shape[1:]
    toks = positions.shape[1]
    rows, feats = cotangent.shape[1:]
    capacity = rows // owners
    taps = conv_weight.shape[1]
    depth = taps * mel
    chans = proj_weight.shape[0]
    quarter = chans // 2
    width = recs * quarter
    assert taps == 3 and toks == LANES == mel and frames == 2 * toks and rows <= 256

    def shift(x, by):
        return lax.ppermute(x, "dp", [(i, (i + by) % recs) for i in range(recs)])

    def swap(x, bit):
        return lax.ppermute(x, "seq", [(i, i ^ bit) for i in range(owners)])

    bit = (seq_index // 2) % 2
    unit = quarter // 64 * 16
    base = core * quarter
    part = (bit * 2 + side) * unit
    part_z = (bit * 2 + 1 - side) * unit
    part_x = ((1 - bit) * 2 + side) * unit
    part_far = ((1 - bit) * 2 + 1 - side) * unit
    cuts = (base + part).reshape(1).astype(I32)
    early = jnp.stack([(j + 1) * quarter + part for j in range(recs - 1)]).astype(I32)
    late = [(j + 1) * quarter + p for p in (part_z, part_x, part_far) for j in range(recs - 1)]
    late = jnp.stack(late).astype(I32)
    offsets = jnp.concatenate([early, late])
    base_in = base.reshape(1).astype(I32)
    bases = jnp.stack([base, (1 - core) * quarter]).astype(I32)
    halves = jnp.stack([(dp_index - j) % recs for j in range(recs)]).astype(I32)
    smem = pl.BlockSpec(memory_space=pltpu.SMEM)
    vmem = pl.BlockSpec(memory_space=pltpu.VMEM)
    hbm = pl.BlockSpec(memory_space=HBM)
    anywhere = pl.BlockSpec(memory_space=pl.ANY)

    high = min(capacity, 8)
    slots = owners * high
    wide_slots = capacity // high * 4 * mel + LANES
    packed, head = call(
        functools.partial(pack_kernel, owners, capacity, rows),
        [
            HBM((slots, wide_slots), BF16),
            pltpu.VMEM((unit, feats), BF16),
        ],
        "pack_patches",
        in_specs=[smem, hbm, hbm, hbm],
        out_specs=[hbm, vmem],
        scratch_shapes=[
            pltpu.VMEM((slots, wide_slots), BF16),
            pltpu.VMEM((frames, mel), BF16),
            pltpu.VMEM((1, toks), I32),
            pltpu.SemaphoreType.DMA((4,)),
        ],
    )(cuts, in_hbm(mel_frames[0]), in_hbm(positions), in_hbm(proj_weight))
    heads = [shift(head, j) for j in range(1, recs)]
    by_z = [swap(h, 4) for h in heads]
    by_x = [swap(h, 2) for h in heads]
    weight_in, _ = lax.optimization_barrier((proj_weight, packed))
    far = lax.dynamic_slice_in_dim(weight_in, base + part_far, unit, 0)
    if extra := quarter - 4 * unit:
        last = lax.dynamic_slice_in_dim(weight_in, base + 4 * unit, extra, 0)
        far = jnp.concatenate([far, last], axis=0)
    cot_in, _ = lax.optimization_barrier((cotangent[0], packed))
    late_weights = by_z + by_x + [shift(far, j) for j in range(1, recs)]
    cot_own = in_hbm(cot_in)
    cot_other = swap(cot_in, 1)

    arrived = lax.all_to_all(
        packed.reshape(owners, high, -1), "seq", split_axis=0, concat_axis=0, tiled=True
    ).reshape(slots, -1)
    def mine(x):
        starts = [(halves[j] * 2 + core) * quarter for j in range(recs)]
        return jnp.concatenate(
            [lax.dynamic_slice_in_dim(x, at, quarter, 1) for at in starts], axis=1
        )

    conv_in, bias_in, _ = lax.optimization_barrier((conv_weight, conv_bias, heads))
    kernel = mine(jnp.transpose(conv_in, (1, 0, 2)).reshape(depth, -1))
    bias = mine(bias_in[None, :])
    share = mel // owners
    wide = share % 8 == 0
    packet = (recs, owners, share, taps * quarter) if wide else (recs, depth, quarter)
    arrived, kernel, bias = lax.optimization_barrier((arrived, kernel, bias))
    arrived_other = swap(arrived, 1)

    early_lanes = quarter // LANES * LANES
    cots, whole, left, slopes, pooled, valid, *ahead = call(
        functools.partial(prepare_kernel, share),
        [
            pltpu.VMEM((2 * rows, feats), BF16),
            pltpu.VMEM((width, feats), BF16),
            pltpu.VMEM((depth, 2 * rows), BF16),
            pltpu.VMEM((2, rows, width), F32),
            pltpu.VMEM((rows, width), BF16),
            pltpu.VMEM((rows, LANES), F32),
        ]
        + (
            [pltpu.VMEM((depth, early_lanes), F32), pltpu.VMEM((rows, early_lanes), BF16)]
            if early_lanes
            else []
        ),
        "prepare",
        in_specs=[smem, smem] + [vmem] * 3 + [anywhere, vmem, anywhere] + [vmem] * len(heads),
        out_specs=[vmem] * (8 if early_lanes else 6),
        scratch_shapes=[pltpu.SemaphoreType.DMA((2,))],
    )(base_in, early, arrived, kernel, bias, cot_own, cot_other, in_hbm(proj_weight), *heads)

    sums, pooled_other = call(
        functools.partial(backward_kernel, share, early_lanes),
        [HBM(packet, BF16), HBM((rows, width), BF16)],
        "backward",
        in_specs=[smem, smem] + [vmem] * (7 + len(ahead) + len(late_weights)),
        out_specs=[hbm, hbm],
        scratch_shapes=[
            pltpu.VMEM((width - early_lanes, feats), BF16),
            pltpu.VMEM(packet, BF16),
            pltpu.VMEM((rows, width), BF16),
            pltpu.VMEM((depth, 2 * rows), BF16),
            pltpu.VMEM((2, rows, width), F32),
            pltpu.SemaphoreType.DMA((1 + recs,)),
        ],
    )(late, halves, cots, whole, left, slopes, kernel, bias, arrived_other, *ahead, *late_weights)
    pieces = lax.all_to_all(
        sums.reshape((recs * owners, -1, packet[-1])),
        ("dp", "seq"),
        split_axis=0,
        concat_axis=0,
        tiled=True,
    )
    foreign = heads + late_weights
    merged = call(
        functools.partial(merge_kernel, quarter),
        HBM((rows, feats), BF16),
        "merge",
        in_specs=[smem, smem] + [vmem] * 4 + [anywhere] * (1 + 2 * len(foreign)),
        scratch_shapes=[
            pltpu.VMEM((2, width, feats), BF16),
            pltpu.SemaphoreType.DMA((2 + 4 * len(foreign),)),
        ],
    )(
        bases,
        offsets,
        pooled,
        swap(pooled_other, 1),
        valid,
        proj_bias[None, :],
        in_hbm(proj_weight),
        *foreign,
        *[swap(w, 1) for w in foreign],
    )
    pieces, merged = lax.optimization_barrier((pieces, merged))
    grad_weight = call(
        functools.partial(sum_kernel, quarter),
        jax.ShapeDtypeStruct((taps * share, chans), F32),
        "sum_pieces",
    )(pieces)
    grad_weight = jnp.transpose(grad_weight.reshape(taps, share, chans), (1, 0, 2))
    return merged[None], grad_weight


def solution(mesh):
    in_specs = (
        P("dp", "seq", None),
        P("dp", "seq"),
        P(),
        P(),
        P("dp", None),
        P(),
        P("dp", "seq", None),
    )
    out_specs = (P("dp", "seq", None), P("seq", None, "dp"))
    return jax.shard_map(body, mesh=mesh, in_specs=in_specs, out_specs=out_specs, check_vma=False)
```
